128 devices in a mesh: grp: 8 (over y, core), leaf: 16 (over z, x).
Axes of the slice: x: 4, y: 4, z: 4, core: 2. Of those that a mesh axis runs over, the one named last changes fastest.
Arguments:
- points: float32 [3, 524288], P(None, ('grp', 'leaf')), as said below
- rhs: float32 [8, 524288], P(None, ('grp', 'leaf')), may hold values from -8 to 8
- start: float32 [8, 524288], P(None, ('grp', 'leaf')), may hold values from -0.6 to 0.6
- leaf_skel: float32 [3, 131072], P(None, ('grp', 'leaf')), as said below
- mid_skel: float32 [3, 8192], P(None, ('grp', 'leaf')), as said below
- top_skel: float32 [3, 512], replicated, as said below
- leaf_basis: float32 [2048, 64, 256], P(('grp', 'leaf')), may hold values from -0.375 to 0.375
- leaf_transfer: float32 [2048, 64, 64], P(('grp', 'leaf')), may hold values from -0.75 to 0.75
- mid_transfer: float32 [128, 64, 64], P(('grp', 'leaf')), may hold values from -0.75 to 0.75
- noise: float32 [1], replicated, may hold values from 0.5 to 2
- near: int32 [2048, 16], P(('grp', 'leaf')), may hold values from 0 to 47, as said below
- near_count: int32 [2048], P(('grp', 'leaf')), may hold values from 1 to 16, as said below
- far_leaf: int32 [2048, 32], P(('grp', 'leaf')), may hold values from 0 to 255, as said below
- far_leaf_count: int32 [2048], P(('grp', 'leaf')), may hold values from 1 to 32, as said below
- far_mid: int32 [128, 16], P(('grp', 'leaf')), may hold values from 0 to 127, as said below
- far_top: int32 [8, 3], P('grp'), may hold values from 0 to 7, as said below
Outputs:
- updated: float32 [8, 524288], P(None, ('grp', 'leaf'))
- residual: float32 [8, 524288], P(None, ('grp', 'leaf'))
The draws below stay inside these ranges and needn't reach their ends.
Inputs may be any that keep to these rules, and one draw needn't show every extreme that they name: `points`: leaves lie in unit boxes on an integer grid in Morton order; every point and skeleton point lies in a box of a leaf of its cluster. `leaf_skel`: skeleton points of a leaf lie in its box. `mid_skel`: skeleton points of a middle cluster lie in boxes of its leaves. `top_skel`: skeleton points of a top cluster lie in boxes of its leaves. `near`: the index j = (l // 16 - 1) * 16 + entry always names a leaf; slot 0 of row l is l itself; the leaves of a row are distinct. `near_count`: some leaf of every device uses all slots. `far_leaf`: entries name leaves of the row's own top cluster, never the row's leaf; distinct within a row. `far_leaf_count`: some leaf of every device uses all slots. `far_mid`: distinct within a row, never the row's own cluster. `far_top`: distinct within a row, never the row's own cluster.
All inputs are finite; a program needn't handle non-finite values.
Results may differ from the reference program's by a relative error of at most 0.0003.
Values sent between devices are 32-bit elements; how exact they have to be, the bound alone decides.
A program may use at most 64 MiB of HBM per device.

```python
import math
import jax
import jax.numpy as jnp
from jax import lax

LEAF_SIZE = 256
BASIS_RANK = 64
RHS_COUNT = 8
LEAF_DEV = 16
NEAR_SLOTS = 16
FAR_LEAF = 32
FAR_MID = 16
FAR_TOP = 3
LEAVES = 2048
POINTS = 524288
MID_CLUSTERS = 128
TOP_CLUSTERS = 8
GROUP_MIDS = 16
GROUP_LEAVES = 256


def morton_corner(leaf_ids):
    coords = [jnp.zeros_like(leaf_ids) for axis_id in range(3)]
    for bit_id in range(30):
        axis_id = bit_id % 3
        picked = jnp.bitwise_and(jnp.right_shift(leaf_ids, bit_id), 1)
        coords[axis_id] = coords[axis_id] + jnp.left_shift(picked, bit_id // 3)
    return jnp.stack(coords).astype(jnp.float32)


def skeleton_points(key, clusters, span, power):
    first_key, second_key = jax.random.split(key)
    total = clusters * BASIS_RANK
    owners = jnp.arange(total, dtype=jnp.int32) // BASIS_RANK
    leaf_ids = owners * span + jax.random.randint(first_key, (total,), 0, span)
    offsets = jax.random.uniform(second_key, (3, total), jnp.float32)
    return morton_corner(leaf_ids) + offsets ** power


def distinct_lists(key, valid, take):
    rows, width = valid.shape
    columns = jnp.arange(width, dtype=jnp.int32)
    scores = jax.random.randint(key, (rows, width), 0, 65536) * width + columns[None, :]
    scores = jnp.where(valid, scores, 1073741824 + columns[None, :])
    order = jnp.argsort(scores, axis=1, stable=True)
    return order[:, :take].astype(jnp.int32)


def ragged_counts(key, most):
    first_key, second_key, third_key = jax.random.split(key, 3)
    leaf_ids = jnp.arange(LEAVES, dtype=jnp.int32)
    owners = leaf_ids // LEAF_DEV
    lowest = jax.random.randint(first_key, (MID_CLUSTERS,), 1, most + 1)
    counts = jax.random.randint(second_key, (LEAVES,), lowest[owners], most + 1)
    full_slot = jax.random.randint(third_key, (MID_CLUSTERS,), 0, LEAF_DEV)
    return jnp.where(leaf_ids % LEAF_DEV == full_slot[owners], most, counts).astype(jnp.int32)


def draw_points(key, part):
    key = jax.random.fold_in(key, 1)
    leaf_ids = jnp.arange(POINTS, dtype=jnp.int32) // LEAF_SIZE
    offsets = jax.random.uniform(key, (3, POINTS), jnp.float32)
    return morton_corner(leaf_ids) + offsets


def draw_rhs(key, part):
    key = jax.random.fold_in(key, 2)
    ramp = 0.6 + 1.4 * jnp.arange(POINTS, dtype=jnp.float32) / POINTS
    values = jnp.clip(jax.random.normal(key, (RHS_COUNT, POINTS), jnp.float32), -4.0, 4.0)
    return values * ramp[None, :]


def draw_leaf_skel(key, part):
    key = jax.random.fold_in(key, 3)
    return skeleton_points(key, LEAVES, 1, 1.0)


def draw_mid_skel(key, part):
    key = jax.random.fold_in(key, 4)
    return skeleton_points(key, MID_CLUSTERS, LEAF_DEV, 1.0)


def draw_top_skel(key, part):
    key = jax.random.fold_in(key, 5)
    return skeleton_points(key, TOP_CLUSTERS, GROUP_LEAVES, 1.0)


def draw_near(key, part):
    key = jax.random.fold_in(key, 6)
    leaf_ids = jnp.arange(LEAVES, dtype=jnp.int32)
    owners = leaf_ids // LEAF_DEV
    itself = LEAF_DEV + leaf_ids % LEAF_DEV
    window = jnp.arange(3 * LEAF_DEV, dtype=jnp.int32)
    global_ids = (owners[:, None] - 1) * LEAF_DEV + window[None, :]
    valid = (global_ids >= 0) & (global_ids < LEAVES) & (window[None, :] != itself[:, None])
    others = distinct_lists(key, valid, NEAR_SLOTS - 1)
    return jnp.concatenate([itself[:, None], others], axis=1).astype(jnp.int32)


def draw_near_count(key, part):
    key = jax.random.fold_in(key, 7)
    return ragged_counts(key, NEAR_SLOTS)


def draw_far_leaf(key, part):
    key = jax.random.fold_in(key, 8)
    leaf_ids = jnp.arange(LEAVES, dtype=jnp.int32)
    columns = jnp.arange(GROUP_LEAVES, dtype=jnp.int32)
    valid = columns[None, :] != (leaf_ids % GROUP_LEAVES)[:, None]
    return distinct_lists(key, valid, FAR_LEAF)


def draw_far_leaf_count(key, part):
    key = jax.random.fold_in(key, 9)
    return ragged_counts(key, FAR_LEAF)


def draw_far_mid(key, part):
    key = jax.random.fold_in(key, 10)
    columns = jnp.arange(MID_CLUSTERS, dtype=jnp.int32)
    valid = columns[None, :] != columns[:, None]
    return distinct_lists(key, valid, FAR_MID)


def draw_far_top(key, part):
    key = jax.random.fold_in(key, 11)
    columns = jnp.arange(TOP_CLUSTERS, dtype=jnp.int32)
    valid = columns[None, :] != columns[:, None]
    return distinct_lists(key, valid, FAR_TOP)


def block_levels(rng, shape, cuts, smallest, largest):
    level = 1.0
    for dim, blocks in cuts:
        draws = jax.random.uniform(jax.random.fold_in(jax.random.fold_in(rng, 6), dim), (blocks,), jnp.float32, smallest / len(cuts), largest / len(cuts))
        level = level * jnp.repeat(jnp.exp(draws), shape[dim] // blocks).reshape((-1,) + (1,) * (len(shape) - 1 - dim))
    return level


def gaussian(key, dims, scale, most, cuts=(), held_as=jnp.bfloat16):
    level = block_levels(key, dims, cuts, -0.22, 0.18) if cuts else 1.0
    result = jax.random.normal(key, dims, jnp.float32) * scale * level
    return jnp.minimum(jnp.maximum(result, -most), most).astype(held_as)


def setup_inputs(seed: int = 0) -> dict:
    keys = jax.random.split(jax.random.key(seed), 17)
    return {
        "points": draw_points(jax.random.fold_in(keys[16], 71), 0),
        "rhs": draw_rhs(jax.random.fold_in(keys[16], 71), 0),
        "start": gaussian(keys[2], (RHS_COUNT, POINTS), 0.1, 0.6, ((1, 128),), jnp.float32),
        "leaf_skel": draw_leaf_skel(jax.random.fold_in(keys[16], 71), 0),
        "mid_skel": draw_mid_skel(jax.random.fold_in(keys[16], 71), 0),
        "top_skel": draw_top_skel(jax.random.fold_in(keys[16], 71), 0),
        "leaf_basis": gaussian(keys[6], (LEAVES, BASIS_RANK, LEAF_SIZE), LEAF_SIZE ** -0.5, 0.375, ((0, 128),), jnp.float32),
        "leaf_transfer": gaussian(keys[7], (LEAVES, BASIS_RANK, BASIS_RANK), BASIS_RANK ** -0.5, 0.75, ((0, 128),), jnp.float32),
        "mid_transfer": gaussian(keys[8], (MID_CLUSTERS, BASIS_RANK, BASIS_RANK), BASIS_RANK ** -0.5, 0.75, ((0, 128),), jnp.float32),
        "noise": jnp.clip(jnp.exp(jax.random.uniform(keys[9], (1,), jnp.float32, math.log(0.5), math.log(2.0))), 0.5, 2.0),
        "near": draw_near(jax.random.fold_in(keys[16], 71), 0),
        "near_count": draw_near_count(jax.random.fold_in(keys[16], 71), 0),
        "far_leaf": draw_far_leaf(jax.random.fold_in(keys[16], 71), 0),
        "far_leaf_count": draw_far_leaf_count(jax.random.fold_in(keys[16], 71), 0),
        "far_mid": draw_far_mid(jax.random.fold_in(keys[16], 71), 0),
        "far_top": draw_far_top(jax.random.fold_in(keys[16], 71), 0),
    }


ROOT_THREE = 1.7320508075688772
LENGTH_SCALE = 2.0

def matern(targets, sources):
    squared = (targets[0][..., :, None] - sources[0][..., None, :]) ** 2
    squared = squared + (targets[1][..., :, None] - sources[1][..., None, :]) ** 2
    squared = squared + (targets[2][..., :, None] - sources[2][..., None, :]) ** 2
    scaled = jnp.sqrt(squared) * (ROOT_THREE / LENGTH_SCALE)
    return (1.0 + scaled) * jnp.exp(-scaled)

def product(form, left, right):
    return jnp.einsum(form, left, right, precision=lax.Precision.HIGHEST)

def near_field(values, points, near, near_count):
    width = LEAF_DEV * LEAF_SIZE
    padded_points = jnp.pad(points, ((0, 0), (width, width)))
    padded_values = jnp.pad(values, ((0, 0), (width, width)))

    def one_device(device_id):
        first = (device_id * width).astype(jnp.int32)
        window_points = lax.dynamic_slice_in_dim(padded_points, first, 3 * width, 1).reshape(3, 3 * LEAF_DEV, LEAF_SIZE)
        window_values = lax.dynamic_slice_in_dim(padded_values, first, 3 * width, 1).reshape(RHS_COUNT, 3 * LEAF_DEV, LEAF_SIZE)
        row_first = (device_id * LEAF_DEV).astype(jnp.int32)
        lists = lax.dynamic_slice_in_dim(near, row_first, LEAF_DEV, 0)
        counts = lax.dynamic_slice_in_dim(near_count, row_first, LEAF_DEV, 0)
        target_points = window_points[:, LEAF_DEV:2 * LEAF_DEV]

        def add_slot(slot_id, total):
            sources = lists[:, slot_id]
            tiles = matern(target_points, window_points[:, sources])
            live = (slot_id < counts).astype(jnp.float32)
            return total + live[None, :, None] * product('lpq,rlq->rlp', tiles, window_values[:, sources])
        start_total = jnp.zeros((RHS_COUNT, LEAF_DEV, LEAF_SIZE), jnp.float32)
        return lax.fori_loop(0, NEAR_SLOTS, add_slot, start_total)
    parts = lax.map(one_device, jnp.arange(MID_CLUSTERS, dtype=jnp.int32))
    return jnp.transpose(parts, (1, 0, 2, 3)).reshape(RHS_COUNT, POINTS)

def apply_operator(values, points, leaf_skel, mid_skel, top_skel, leaf_basis, leaf_transfer, mid_transfer, noise, near, near_count, far_leaf, far_leaf_count, far_mid, far_top):
    blocks = values.reshape(RHS_COUNT, LEAVES, LEAF_SIZE)
    leaf_coef = product('lkp,rlp->lrk', leaf_basis, blocks)
    mid_coef = product('lij,lrj->lri', leaf_transfer, leaf_coef).reshape(MID_CLUSTERS, LEAF_DEV, RHS_COUNT, BASIS_RANK).sum(1)
    top_coef = product('mij,mrj->mri', mid_transfer, mid_coef).reshape(TOP_CLUSTERS, GROUP_MIDS, RHS_COUNT, BASIS_RANK).sum(1)
    leaf_points = leaf_skel.reshape(3, LEAVES, BASIS_RANK)
    mid_points = mid_skel.reshape(3, MID_CLUSTERS, BASIS_RANK)
    top_points = top_skel.reshape(3, TOP_CLUSTERS, BASIS_RANK)
    bases = jnp.arange(LEAVES, dtype=jnp.int32) // GROUP_LEAVES * GROUP_LEAVES

    def add_far(slot_id, total):
        sources = bases + far_leaf[:, slot_id]
        tiles = matern(leaf_points, leaf_points[:, sources])
        live = (slot_id < far_leaf_count).astype(jnp.float32)
        return total + live[:, None, None] * product('lij,lrj->lri', tiles, leaf_coef[sources])
    leaf_far = lax.fori_loop(0, FAR_LEAF, add_far, jnp.zeros((LEAVES, RHS_COUNT, BASIS_RANK), jnp.float32))
    mid_tiles = matern(mid_points[:, :, None, :], mid_points[:, far_mid])
    mid_far = product('mfij,mfrj->mri', mid_tiles, mid_coef[far_mid])
    top_tiles = matern(top_points[:, :, None, :], top_points[:, far_top])
    top_far = product('gfij,gfrj->gri', top_tiles, top_coef[far_top])
    mid_local = mid_far + product('mji,mrj->mri', mid_transfer, jnp.repeat(top_far, GROUP_MIDS, axis=0))
    leaf_local = leaf_far + product('lji,lrj->lri', leaf_transfer, jnp.repeat(mid_local, LEAF_DEV, axis=0))
    far_part = product('lkp,lrk->rlp', leaf_basis, leaf_local).reshape(RHS_COUNT, POINTS)
    return noise[0] * values + near_field(values, points, near, near_count) + far_part

def reference(points, rhs, start, leaf_skel, mid_skel, top_skel, leaf_basis, leaf_transfer, mid_transfer, noise, near, near_count, far_leaf, far_leaf_count, far_mid, far_top):

    def operator(values):
        return apply_operator(values, points, leaf_skel, mid_skel, top_skel, leaf_basis, leaf_transfer, mid_transfer, noise, near, near_count, far_leaf, far_leaf_count, far_mid, far_top)
    first_residual = rhs - operator(start)
    image = operator(first_residual)
    numerator = lax.optimization_barrier(jnp.mean(first_residual * image, axis=1))
    denominator = lax.optimization_barrier(jnp.mean(image * image, axis=1)) + 1e-06
    alpha = numerator / denominator
    updated = start + alpha[:, None] * first_residual
    residual = first_residual - alpha[:, None] * image
    return (updated, residual)
```

```python
import functools
import math

import jax
import jax.numpy as jnp
import numpy as np
from jax import lax
from jax.experimental import pallas as pl
from jax.experimental.pallas import tpu as pltpu
from jax.sharding import PartitionSpec as P

BF = jnp.bfloat16
F32 = jnp.float32
MESH = pl.DeviceIdType.MESH
NT = (((1,), (1,)), ((), ()))

LEAF = 256
RANK = 64
RHS = 8
PER = 16
NEAR = 16
FARL = 32
FARM = 16
FART = 3
GROUPS = 8
GSIZE = 16
LEAVES = 2048
WIN = 3 * PER
PIECES = 48
UNROLL = 4

LOG2E = math.log2(math.e)
KAPPA = 0.75 * LOG2E * LOG2E
FACTOR = math.e * math.log(2.0)
TINY = 1e-30


def morton_table():
    ids = np.arange(LEAVES)
    coords = [np.zeros_like(ids) for _ in range(3)]
    for bit in range(30):
        coords[bit % 3] += ((ids >> bit) & 1) << (bit // 3)
    packed = coords[0] + 256 * coords[1] + 65536 * coords[2]
    return np.pad(packed, (PER, PER)).astype(np.int32)


def tangent_tables():
    mean = 0.75 * (np.arange(512) + 0.5)
    s = np.sqrt(mean)
    beta = 0.5 * np.exp(-s) / (LOG2E * LOG2E) / FACTOR
    alpha = -(1 + s) * np.exp(-s) / FACTOR - beta * mean * LOG2E * LOG2E
    return alpha.astype(np.float32), beta.astype(np.float32)


def rounded(x):
    return x.astype(BF).astype(F32)


def split2(x):
    high = rounded(x)
    return jnp.concatenate([high, x - high], axis=0).astype(BF)


def split3(x):
    first = rounded(x)
    rest = x - first
    second = rounded(rest)
    return first, second, rounded(rest - second)


def source_pieces(w):
    a, b, c = split3(w)
    return jnp.concatenate([a, b, a, b, c, a], axis=0)


def target_pieces(u):
    a, b, c = split3(u)
    return jnp.concatenate([a, a, b, b, a, c], axis=0)


def rows_of(shape):
    return lax.broadcasted_iota(jnp.int32, shape, 0)


def source_rows(x):
    row = rows_of(x.shape)
    x = jnp.where(row < 3, x, 0.0)
    norm = KAPPA * jnp.sum(x * x, axis=0, keepdims=True)
    return jnp.where(row == 3, norm, jnp.where(row == 4, 1.0, x))


def target_rows(x):
    row = rows_of(x.shape)
    x = jnp.where(row < 3, x, 0.0)
    norm = KAPPA * jnp.sum(x * x, axis=0, keepdims=True)
    return jnp.where(row == 4, norm, jnp.where(row == 3, 1.0, (-2.0 * KAPPA) * x))


def kernel_value(q):
    q = jnp.maximum(q, TINY)
    y = -LOG2E - q * lax.rsqrt(q)
    return y * jnp.exp2(y)


def halves(x):
    high = x.astype(BF)
    return high, (x - high.astype(F32)).astype(BF)


def dot(a, b):
    return jnp.dot(a, b, preferred_element_type=F32)


def dot_nt(a, b):
    return lax.dot_general(a, b, NT, preferred_element_type=F32)


def fold(x):
    return x[:RHS] + x[RHS:]


def body(
    points,
    rhs,
    start,
    leaf_skel,
    mid_skel,
    top_skel,
    basis,
    transfer,
    mid_transfer,
    noise,
    near,
    near_count,
    far_leaf,
    far_count,
    far_mid,
    far_top,
    corners,
    alphas,
    betas,
    updated,
    residual,
    remainder,
    qa,
    qb,
    far_high,
    far_low,
    mid_high,
    mid_low,
    top_high,
    top_low,
    halo1,
    halo2,
    gather1,
    gather2,
    mids1,
    mids2,
    all1,
    all2,
    sums1,
    sums2,
    field,
    wfeat,
    ufeat,
    wrows,
    urows,
    moments,
    skel_feat,
    mid_feat,
    top_feat,
    top_tiles,
    basis_high,
    basis_low,
    transfer2,
    near_acc,
    local,
    image,
    first,
    halo_send,
    halo_recv,
    mid_send,
    mid_recv,
    coef_send,
    coef_recv,
    all_send,
    all_recv,
    sum_send,
    sum_recv,
    tot_send,
    tot_recv,
):
    g = lax.axis_index("grp")
    i = lax.axis_index("leaf")
    lane = lax.broadcasted_iota(jnp.int32, (RHS, 128), 1)
    low_lanes = lane < RANK

    def peer_leaf(k):
        return (g, lax.rem(i + k, GSIZE))

    def peer_grp(k):
        return (lax.rem(g + k, GROUPS), i)

    up = i + 1
    down = i + GSIZE - 1
    after = (lax.rem(g + lax.div(up, GSIZE), GROUPS), lax.rem(up, GSIZE))
    before = (lax.rem(g + GROUPS - 1 + lax.div(down, GSIZE), GROUPS), lax.rem(down, GSIZE))

    barrier = pltpu.get_barrier_semaphore()
    partners = (
        [peer_leaf(k) for k in range(1, GSIZE)]
        + [peer_grp(k) for k in range(1, GROUPS)]
        + [after, before]
    )
    for partner in partners:
        pl.semaphore_signal(barrier, inc=1, device_id=partner, device_id_type=MESH)

    def remote(src, dst, send, recv, device):
        return pltpu.make_async_remote_copy(
            src_ref=src,
            dst_ref=dst,
            send_sem=send,
            recv_sem=recv,
            device_id=device,
            device_id_type=MESH,
        )

    def halo_copies(window, phase):
        own = window.at[1]
        return [
            remote(own, window.at[0], halo_send.at[phase, 0], halo_recv.at[phase, 0], after),
            remote(own, window.at[2], halo_send.at[phase, 1], halo_recv.at[phase, 1], before),
        ]

    def leaf_copies(buffer, send, recv, phase):
        return [
            remote(buffer.at[i], buffer.at[i], send.at[phase, k], recv.at[phase, i], peer_leaf(k))
            for k in range(1, GSIZE)
        ]

    def wait_leaf(buffer, send, recv, phase):
        for k in range(1, GSIZE):
            src = lax.rem(i + k, GSIZE)
            remote(
                buffer.at[src], buffer.at[src], send.at[phase, k], recv.at[phase, src], peer_leaf(k)
            ).wait_recv()

    def grp_copies(buffer, send, recv, phase):
        return [
            remote(buffer.at[g], buffer.at[g], send.at[phase, k], recv.at[phase, g], peer_grp(k))
            for k in range(1, GROUPS)
        ]

    def wait_grp(buffer, send, recv, phase):
        for k in range(1, GROUPS):
            src = lax.rem(g + k, GROUPS)
            remote(
                buffer.at[src], buffer.at[src], send.at[phase, k], recv.at[phase, src], peer_grp(k)
            ).wait_recv()

    pending = []

    def launch(copies):
        for copy in copies:
            copy.start()
        pending.extend(copies)

    def coefficients(read, tiles, mid_tile):
        def pair(p, carry):
            parts = []
            for side in range(2):
                leaf = 2 * p + side
                v = split2(read(leaf))
                field[PER + leaf] = v
                both = dot_nt(v, basis_high[leaf]) + dot_nt(v, basis_low[leaf])
                parts.append(fold(both))
            tiles[p] = jnp.concatenate(parts, axis=1)
            return carry

        lax.fori_loop(0, PER // 2, pair, 0)
        total = jnp.zeros((2 * RHS, RANK), F32)
        for p in range(PER // 2):
            c = split2(tiles[p])
            for part in range(2):
                total += dot_nt(c, transfer2[part, :, 128 * p : 128 * (p + 1)])
        mid = fold(total)
        m = split2(mid)
        own = mid_transfer[0]
        high, low = halves(own)
        top = fold(dot_nt(m, high) + dot_nt(m, low))
        mid_tile[...] = jnp.concatenate([mid, top], axis=1)

    for leaf in range(PER):
        high, low = halves(basis[leaf])
        basis_high[leaf] = high
        basis_low[leaf] = low
    for p in range(PER // 2):
        both = jnp.concatenate([transfer[2 * p], transfer[2 * p + 1]], axis=1)
        high, low = halves(both)
        transfer2[0, :, 128 * p : 128 * (p + 1)] = high
        transfer2[1, :, 128 * p : 128 * (p + 1)] = low

    halo1[1, 0] = jnp.zeros((8, PER * LEAF), F32)
    halo1[1, 0, 0:3, :] = points[...]
    halo1[1, 1] = start[...]
    own_gather = gather1.at[i]
    for p in range(PER // 2):
        own_gather[PER // 2 + p] = jnp.zeros((8, 128), F32)
        own_gather[PER // 2 + p, 0:3, :] = leaf_skel[:, 128 * p : 128 * (p + 1)]
    mids1[i, 1] = jnp.zeros((8, 128), F32)
    mids1[i, 1, 0:3, 0:RANK] = mid_skel[...]

    def column(leaf):
        return pl.ds(pl.multiple_of(leaf * LEAF, LEAF), LEAF)

    coefficients(lambda leaf: start[:, column(leaf)], gather1.at[i], mids1.at[i, 0])

    pl.semaphore_wait(barrier, len(partners))
    launch(halo_copies(halo1, 0))
    launch(leaf_copies(mids1, mid_send, mid_recv, 0))
    launch(leaf_copies(gather1, coef_send, coef_recv, 0))

    centre = jnp.floor(halo1[1, 0, :, 0:1])

    def window_features(leaf, block, place):
        x = halo1[block, 0, :, column(place)] - centre
        w = source_rows(x)
        wrows[leaf] = w
        wfeat[leaf] = source_pieces(w).T.astype(BF)
        return x

    def own_features(l, carry):
        x = window_features(PER + l, 1, l)
        u = target_rows(x)
        urows[l] = u
        ufeat[l] = target_pieces(u).astype(BF)
        return carry

    lax.fori_loop(0, PER, own_features, 0)
    for p in range(PER // 2):
        u = target_pieces(target_rows(own_gather[PER // 2 + p] - centre))
        skel_feat[128 * p : 128 * (p + 1), :] = u.T.astype(BF)
    u = target_pieces(target_rows(mids1[i, 1] - centre))
    mid_feat[...] = u.T.astype(BF)
    for p in range(GROUPS // 2):
        top_tiles[p] = jnp.zeros((8, 128), F32)
        top_tiles[p, 0:3, :] = top_skel[:, 128 * p : 128 * (p + 1)]
    tile = top_tiles[lax.div(g, 2)]
    tile = jnp.where(lax.rem(g, 2) == 0, tile, pltpu.roll(tile, RANK, 1))
    top_feat[...] = target_pieces(target_rows(tile - centre)).T.astype(BF)

    def window_moments(leaf, v):
        for k in range(5):
            total = jnp.sum(v * wrows[leaf, k : k + 1, :], axis=1, keepdims=True)
            moments[leaf, k] = jnp.broadcast_to(total, (RHS, 128))

    def own_moments(read):
        def one(l, carry):
            window_moments(PER + l, read(l))
            return carry

        lax.fori_loop(0, PER, one, 0)

    own_moments(lambda l: start[:, column(l)])
    for copy in halo_copies(halo1, 0):
        copy.wait_recv()

    def edge_features(l, carry):
        for block in (0, 2):
            leaf = block * PER + l
            window_features(leaf, block, l)
            v = halo1[block, 1, :, column(l)]
            field[leaf] = split2(v)
            window_moments(leaf, v)
        return carry

    lax.fori_loop(0, PER, edge_features, 0)

    wait_leaf(mids1, mid_send, mid_recv, 0)
    all1[g] = mids1[...]
    launch(grp_copies(all1, all_send, all_recv, 0))

    device = g * GSIZE + i
    base = device * PER

    def distance2(l, s):
        a = corners[base + PER + l]
        b = corners[base + near[l, s]]
        dx = (a & 255) - (b & 255)
        dy = ((a >> 8) & 255) - ((b >> 8) & 255)
        dz = (a >> 16) - (b >> 16)
        return jnp.minimum(dx * dx + dy * dy + dz * dz, 511)

    def fill(ref, l, s0):
        for t in range(UNROLL):
            ref[t] = dot(wfeat[near[l, s0 + t]], ufeat[l])

    def evaluate(ref, l, s0):
        for t in range(UNROLL):
            d2 = distance2(l, s0 + t)
            alpha, beta = alphas[d2], betas[d2]
            for c in range(0, LEAF, 64):
                q = ref[t, c : c + 64, :]
                r = kernel_value(q) - (q * beta + alpha)
                remainder[l * NEAR + s0 + t, c : c + 64, :] = r.astype(BF)

    def multiply(l, s0, count):
        total = jnp.zeros((2 * RHS, LEAF), F32)
        for t in range(count):
            s = s0 + t
            v = field[near[l, s]]
            v = jnp.where(s < near_count[l], v, jnp.zeros_like(v))
            total += dot(v, remainder[l * NEAR + s])
        return total

    def tangent_part(l):
        sums = [jnp.zeros((RHS, 128), F32) for _ in range(5)]
        for s in range(NEAR):
            d2 = distance2(l, s)
            live = jnp.where(s < near_count[l], 1.0, 0.0)
            alpha, beta = alphas[d2] * live, betas[d2] * live
            j = near[l, s]
            for k in range(5):
                sums[k] += beta * moments[j, k]
            sums[3] += alpha * moments[j, 4]
        total = jnp.zeros((RHS, LEAF), F32)
        for k in range(5):
            c = jnp.concatenate([sums[k], sums[k]], axis=1)
            total += c * urows[l, k : k + 1, :]
        return total

    steps = PER * NEAR // UNROLL
    per_leaf = NEAR // UNROLL

    def place(step):
        return lax.div(step, per_leaf), lax.rem(step, per_leaf) * UNROLL

    near_acc[...] = jnp.zeros((PER, 2 * RHS, LEAF), F32)
    fill(qa, 0, 0)

    def near_step(n, carry):
        step = 2 * n
        l0, s0 = place(step)
        l1, s1 = place(step + 1)
        l2, s2 = place(jnp.minimum(step + 2, steps - 1))
        lp, sp = place(jnp.maximum(step - 1, 0))
        fill(qb, l1, s1)
        evaluate(qa, l0, s0)
        fill(qa, l2, s2)
        near_acc[l0] += multiply(l0, s0, UNROLL)
        evaluate(qb, l1, s1)
        near_acc[l1] += multiply(l1, s1, UNROLL)
        return carry

    lax.fori_loop(0, steps // 2, near_step, 0)

    def picked(read, index, want):
        tile = read(index)
        return jnp.where(lax.rem(index, 2) == want, tile, pltpu.roll(tile, RANK, 1))

    def joined(first_tile, second_tile):
        return jnp.where(low_lanes, first_tile, second_tile)

    def far_tiles(feat, tile):
        w = source_pieces(source_rows(tile - centre)).astype(BF)
        return halves(kernel_value(dot(feat, w)))

    def leaf_tile(buffer, offset):
        def read(j):
            return buffer[lax.div(j, GSIZE), offset + lax.div(lax.rem(j, GSIZE), 2)]

        return read

    def far_matrix(lp, carry):
        read = leaf_tile(gather1, PER // 2)
        for side in range(2):
            l = 2 * lp + side
            feat = skel_feat[pl.ds(pl.multiple_of(l * RANK, RANK), RANK), :]
            for p in range(FARL // 2):
                tile = joined(
                    picked(read, far_leaf[l, 2 * p], 0), picked(read, far_leaf[l, 2 * p + 1], 1)
                )
                high, low = far_tiles(feat, tile)
                far_high[l, :, 128 * p : 128 * (p + 1)] = high
                far_low[l, :, 128 * p : 128 * (p + 1)] = low
        return carry

    def far_leaves(buffer):
        read = leaf_tile(buffer, 0)

        def pair(lp, carry):
            parts = []
            for side in range(2):
                l = 2 * lp + side
                cols = []
                for p in range(FARL // 2):
                    s = 2 * p
                    tile = joined(
                        picked(read, far_leaf[l, s], 0), picked(read, far_leaf[l, s + 1], 1)
                    )
                    count = far_count[l]
                    slot = s + jnp.where(low_lanes, 0, 1)
                    cols.append(split2(jnp.where(slot < count, tile, 0.0)))
                c = jnp.concatenate(cols, axis=1)
                parts.append(fold(dot_nt(c, far_high[l]) + dot_nt(c, far_low[l])))
            local[lp] = -FACTOR * jnp.concatenate(parts, axis=1)
            return carry

        lax.fori_loop(0, PER // 2, pair, 0)

    def upper_matrix(buffer):
        def read_mid(m):
            return buffer[lax.div(m, GSIZE), lax.rem(m, GSIZE), 1]

        for p in range(FARM // 2):
            one, two = read_mid(far_mid[0, 2 * p]), read_mid(far_mid[0, 2 * p + 1])
            high, low = far_tiles(
                mid_feat[0:RANK, :], joined(one, pltpu.roll(two, RANK, 1))
            )
            mid_high[:, 128 * p : 128 * (p + 1)] = high
            mid_low[:, 128 * p : 128 * (p + 1)] = low

        def read_top(j):
            return top_tiles[lax.div(j, 2)]

        for p in range(2):
            j1 = far_top[0, 2 * p]
            j2 = far_top[0, min(2 * p + 1, FART - 1)]
            high, low = far_tiles(
                top_feat[0:RANK, :], joined(picked(read_top, j1, 0), picked(read_top, j2, 1))
            )
            top_high[:, 128 * p : 128 * (p + 1)] = high
            top_low[:, 128 * p : 128 * (p + 1)] = low

    def upper_local(read):
        cols = []
        for p in range(FARM // 2):
            one, two = read(far_mid[0, 2 * p]), read(far_mid[0, 2 * p + 1])
            cols.append(split2(joined(one, pltpu.roll(two, RANK, 1))))
        c = jnp.concatenate(cols, axis=1)
        mid_far = -FACTOR * fold(dot_nt(c, mid_high[...]) + dot_nt(c, mid_low[...]))

        def top(j):
            total = jnp.zeros((RHS, 128), F32)
            for m in range(GSIZE):
                total += read(j * GSIZE + m)
            return total

        t0, t1, t2 = (top(far_top[0, s]) for s in range(FART))
        cols = [
            split2(joined(pltpu.roll(t0, RANK, 1), t1)),
            split2(joined(pltpu.roll(t2, RANK, 1), jnp.zeros((RHS, 128), F32))),
        ]
        c = jnp.concatenate(cols, axis=1)
        top_far = -FACTOR * fold(dot_nt(c, top_high[...]) + dot_nt(c, top_low[...]))
        high, low = halves(mid_transfer[0])
        t = split2(top_far)
        return mid_far + fold(dot(t, high) + dot(t, low))

    def finish(read_mid, store):
        m = split2(upper_local(read_mid))
        for p in range(PER // 2):
            down_part = sum(dot(m, transfer2[part, :, 128 * p : 128 * (p + 1)]) for part in range(2))
            local[p] += fold(down_part)

        def pair(lp, carry):
            tile = local[lp]
            for side in range(2):
                l = 2 * lp + side
                c = split2(tile[:, RANK * side : RANK * (side + 1)])
                far = fold(dot(c, basis_high[l]) + dot(c, basis_low[l]))
                near_part = -FACTOR * (fold(near_acc[l]) + tangent_part(l))
                store(l, near_part + far)
            return carry

        lax.fori_loop(0, PER // 2, pair, 0)

    wait_leaf(gather1, coef_send, coef_recv, 0)
    lax.fori_loop(0, PER // 2, far_matrix, 0)
    far_leaves(gather1)
    wait_grp(all1, all_send, all_recv, 0)
    upper_matrix(all1)
    noise_value = noise[0]

    def store_first(l, value):
        cols = column(l)
        r = rhs[:, cols] - (noise_value * start[:, cols] + value)
        first[l] = r
        halo2[1, :, cols] = r

    finish(lambda m: all1[lax.div(m, GSIZE), lax.rem(m, GSIZE), 0], store_first)

    launch(halo_copies(halo2, 1))
    coefficients(lambda leaf: first[leaf], gather2.at[i], mids2.at[i])
    launch(leaf_copies(mids2, mid_send, mid_recv, 1))
    launch(leaf_copies(gather2, coef_send, coef_recv, 1))
    own_moments(lambda l: first[l])
    for copy in halo_copies(halo2, 1):
        copy.wait_recv()

    def edge_moments(l, carry):
        for block in (0, 2):
            leaf = block * PER + l
            v = halo2[block, :, column(l)]
            field[leaf] = split2(v)
            window_moments(leaf, v)
        return carry

    lax.fori_loop(0, PER, edge_moments, 0)
    wait_leaf(mids2, mid_send, mid_recv, 1)
    all2[g] = mids2[...]
    launch(grp_copies(all2, all_send, all_recv, 1))

    def near_again(l, carry):
        near_acc[l] = multiply(l, 0, NEAR)
        return carry

    lax.fori_loop(0, PER, near_again, 0)
    wait_leaf(gather2, coef_send, coef_recv, 1)
    far_leaves(gather2)
    wait_grp(all2, all_send, all_recv, 1)

    def store_image(l, value):
        image[l] = noise_value * first[l] + value

    finish(lambda m: all2[lax.div(m, GSIZE), lax.rem(m, GSIZE)], store_image)

    dots = jnp.zeros((RHS, LEAF), F32)
    squares = jnp.zeros((RHS, LEAF), F32)
    for l in range(PER):
        dots += first[l] * image[l]
        squares += image[l] * image[l]
    sums1[i] = jnp.where(
        low_lanes,
        jnp.sum(dots, axis=1, keepdims=True),
        jnp.sum(squares, axis=1, keepdims=True),
    )
    launch(leaf_copies(sums1, sum_send, sum_recv, 0))
    wait_leaf(sums1, sum_send, sum_recv, 0)
    total = sums1[0]
    for k in range(1, GSIZE):
        total += sums1[k]
    sums2[g] = total
    launch(grp_copies(sums2, tot_send, tot_recv, 0))
    wait_grp(sums2, tot_send, tot_recv, 0)
    total = sums2[0]
    for k in range(1, GROUPS):
        total += sums2[k]
    total = total / (LEAVES * LEAF)
    alpha = total[:, 0:1] / (total[:, RANK : RANK + 1] + 1e-6)
    for l in range(PER):
        cols = slice(l * LEAF, (l + 1) * LEAF)
        r = first[l]
        updated[:, cols] = start[:, cols] + alpha * r
        residual[:, cols] = r - alpha * image[l]
    for copy in pending:
        copy.wait_send()


def shards(*args):
    smem = pl.BlockSpec(memory_space=pltpu.SMEM)
    vmem = pl.BlockSpec(memory_space=pltpu.VMEM)
    alphas, betas = tangent_tables()
    tables = (jnp.asarray(morton_table()), jnp.asarray(alphas), jnp.asarray(betas))
    out = jax.ShapeDtypeStruct((RHS, PER * LEAF), F32)
    tile = (8, 128)

    def buffer(shape, dtype=F32):
        return pltpu.VMEM(shape, dtype)

    def sems(*shape):
        return pltpu.SemaphoreType.DMA(shape)

    scratch = [
        buffer((PER * NEAR, LEAF, LEAF), BF),
        buffer((UNROLL, LEAF, LEAF)),
        buffer((UNROLL, LEAF, LEAF)),
        buffer((PER, RANK, FARL * RANK), BF),
        buffer((PER, RANK, FARL * RANK), BF),
        buffer((RANK, FARM * RANK), BF),
        buffer((RANK, FARM * RANK), BF),
        buffer((RANK, 4 * RANK), BF),
        buffer((RANK, 4 * RANK), BF),
        buffer((3, 2, 8, PER * LEAF)),
        buffer((3, 8, PER * LEAF)),
        buffer((GSIZE, PER) + tile),
        buffer((GSIZE, PER // 2) + tile),
        buffer((GSIZE, 2) + tile),
        buffer((GSIZE,) + tile),
        buffer((GROUPS, GSIZE, 2) + tile),
        buffer((GROUPS, GSIZE) + tile),
        buffer((GSIZE,) + tile),
        buffer((GROUPS,) + tile),
        buffer((WIN, 2 * RHS, LEAF), BF),
        buffer((WIN, LEAF, PIECES), BF),
        buffer((PER, PIECES, LEAF), BF),
        buffer((WIN, 8, LEAF)),
        buffer((PER, 8, LEAF)),
        buffer((WIN, 5) + tile),
        buffer((PER * RANK, PIECES), BF),
        buffer((128, PIECES), BF),
        buffer((128, PIECES), BF),
        buffer((GROUPS // 2,) + tile),
        buffer((PER, RANK, LEAF), BF),
        buffer((PER, RANK, LEAF), BF),
        buffer((2, RANK, PER * RANK), BF),
        buffer((PER, 2 * RHS, LEAF)),
        buffer((PER // 2,) + tile),
        buffer((PER, RHS, LEAF)),
        buffer((PER, RHS, LEAF)),
        sems(2, 2),
        sems(2, 2),
        sems(2, GSIZE),
        sems(2, GSIZE),
        sems(2, GSIZE),
        sems(2, GSIZE),
        sems(2, GROUPS),
        sems(2, GROUPS),
        sems(1, GSIZE),
        sems(1, GSIZE),
        sems(1, GROUPS),
        sems(1, GROUPS),
    ]
    return pl.pallas_call(
        body,
        out_shape=(out, out),
        in_specs=[vmem] * 9 + [smem] * 10,
        out_specs=(vmem, vmem),
        scratch_shapes=scratch,
        compiler_params=pltpu.CompilerParams(
            collective_id=0, has_side_effects=True, vmem_limit_bytes=61 << 20
        ),
    )(*args, *tables)


def solution(mesh):
    columns = P(None, ("grp", "leaf"))
    blocks = P(("grp", "leaf"), None, None)
    lists = P(("grp", "leaf"), None)
    return jax.shard_map(
        shards,
        mesh=mesh,
        in_specs=(
            columns,
            columns,
            columns,
            columns,
            columns,
            P(),
            blocks,
            blocks,
            blocks,
            P(),
            lists,
            P(("grp", "leaf")),
            lists,
            P(("grp", "leaf")),
            lists,
            P("grp", None),
        ),
        out_specs=(columns, columns),
        check_vma=False,
    )
```

```python
import functools
import math

import jax
import jax.numpy as jnp
import numpy as np
from jax import lax
from jax.experimental import pallas as pl
from jax.experimental.pallas import tpu as pltpu
from jax.sharding import PartitionSpec as P

BF = jnp.bfloat16
F32 = jnp.float32
MESH = pl.DeviceIdType.MESH
NT = (((1,), (1,)), ((), ()))

LEAF = 256
RANK = 64
RHS = 8
PER = 16
NEAR = 16
FARL = 32
FARM = 16
FART = 3
GROUPS = 8
GSIZE = 16
LEAVES = 2048
WIN = 3 * PER
PIECES = 48
TILES1 = 2 + PER
TILES2 = 1 + PER // 2
PACKED = 3 * PER * LEAF // 8

LOG2E = math.log2(math.e)
KAPPA = 0.75 * LOG2E * LOG2E
FACTOR = math.e * math.log(2.0)
TINY = 1e-30


def morton_table():
    ids = np.arange(LEAVES)
    coords = [np.zeros_like(ids) for _ in range(3)]
    for bit in range(30):
        coords[bit % 3] += ((ids >> bit) & 1) << (bit // 3)
    packed = coords[0] + 256 * coords[1] + 65536 * coords[2]
    return np.pad(packed, (PER, PER)).astype(np.int32)


def tangent_tables():
    mean = 0.75 * (np.arange(512) + 0.5)
    s = np.sqrt(mean)
    beta = 0.5 * np.exp(-s) / (LOG2E * LOG2E) / FACTOR
    alpha = -(1 + s) * np.exp(-s) / FACTOR - beta * mean * LOG2E * LOG2E
    return alpha.astype(np.float32), beta.astype(np.float32)


def rounded(x):
    return x.astype(BF).astype(F32)


def split2(x):
    high = rounded(x)
    return jnp.concatenate([high, x - high], axis=0).astype(BF)


def split3(x):
    first = rounded(x)
    rest = x - first
    second = rounded(rest)
    return first, second, rounded(rest - second)


def source_pieces(w):
    a, b, c = split3(w)
    return jnp.concatenate([a, b, a, b, c, a], axis=0)


def target_pieces(u):
    a, b, c = split3(u)
    return jnp.concatenate([a, a, b, b, a, c], axis=0)


def rows_of(shape):
    return lax.broadcasted_iota(jnp.int32, shape, 0)


def source_rows(x):
    row = rows_of(x.shape)
    x = jnp.where(row < 3, x, 0.0)
    norm = KAPPA * jnp.sum(x * x, axis=0, keepdims=True)
    return jnp.where(row == 3, norm, jnp.where(row == 4, 1.0, x))


def target_rows(x):
    row = rows_of(x.shape)
    x = jnp.where(row < 3, x, 0.0)
    norm = KAPPA * jnp.sum(x * x, axis=0, keepdims=True)
    return jnp.where(row == 4, norm, jnp.where(row == 3, 1.0, (-2.0 * KAPPA) * x))


def kernel_value(q):
    q = jnp.maximum(q, TINY)
    y = -LOG2E - q * lax.rsqrt(q)
    return y * jnp.exp2(y)


def halves(x):
    high = x.astype(BF)
    return high, (x - high.astype(F32)).astype(BF)


def dot(a, b):
    return jnp.dot(a, b, preferred_element_type=F32)


def dot_nt(a, b):
    return lax.dot_general(a, b, NT, preferred_element_type=F32)


def fold(x):
    return x[:RHS] + x[RHS:]


def body(
    points,
    rhs,
    start,
    leaf_skel,
    mid_skel,
    top_skel,
    basis,
    transfer,
    mid_transfer,
    noise,
    near,
    near_count,
    far_leaf,
    far_count,
    far_mid,
    far_top,
    corners,
    alphas,
    betas,
    first,
    image,
    step,
    remainder,
    far_high,
    far_low,
    mid_high,
    mid_low,
    top_high,
    top_low,
    halo1,
    halo2,
    gather1,
    gather2,
    all1,
    all2,
    sums1,
    sums2,
    field,
    wfeat,
    ufeat,
    urows,
    moments,
    skel_rows,
    tangent_a,
    tangent_b,
    skel_feat,
    mid_feat,
    top_feat,
    top_tiles,
    basis_high,
    basis_low,
    transfer2,
    near_acc,
    local,
    halo_send,
    halo_recv,
    coef_send,
    coef_recv,
    all_send,
    all_recv,
    sum_send,
    sum_recv,
    tot_send,
    tot_recv,
):
    g = lax.axis_index("grp")
    i = lax.axis_index("leaf")
    lane = lax.broadcasted_iota(jnp.int32, (RHS, 128), 1)
    low_lanes = lane < RANK

    def peer_leaf(k):
        return (g, lax.rem(i + k, GSIZE))

    def peer_grp(k):
        return (lax.rem(g + k, GROUPS), i)

    up = i + 1
    down = i + GSIZE - 1
    after = (lax.rem(g + lax.div(up, GSIZE), GROUPS), lax.rem(up, GSIZE))
    before = (lax.rem(g + GROUPS - 1 + lax.div(down, GSIZE), GROUPS), lax.rem(down, GSIZE))

    barrier = pltpu.get_barrier_semaphore()
    partners = (
        [peer_leaf(k) for k in range(1, GSIZE)]
        + [peer_grp(k) for k in range(1, GROUPS)]
        + [after, before]
    )
    for partner in partners:
        pl.semaphore_signal(barrier, inc=1, device_id=partner, device_id_type=MESH)

    def remote(src, dst, send, recv, device):
        return pltpu.make_async_remote_copy(
            src_ref=src,
            dst_ref=dst,
            send_sem=send,
            recv_sem=recv,
            device_id=device,
            device_id_type=MESH,
        )

    def halo_copies(window, phase, *where):
        own, low, high = (window.at[(block,) + where] for block in (1, 0, 2))
        return [
            remote(own, low, halo_send.at[phase, 0], halo_recv.at[phase, 0], after),
            remote(own, high, halo_send.at[phase, 1], halo_recv.at[phase, 1], before),
        ]

    def leaf_copies(buffer, send, recv, phase):
        own = buffer.at[i]
        return [
            remote(own, own, send.at[phase, k], recv.at[phase, i], peer_leaf(k))
            for k in range(1, GSIZE)
        ]

    def wait_leaf(buffer, send, recv, phase):
        for k in range(1, GSIZE):
            src = lax.rem(i + k, GSIZE)
            theirs = buffer.at[src]
            remote(theirs, theirs, send.at[phase, k], recv.at[phase, src], peer_leaf(k)).wait_recv()

    def grp_copies(buffer, send, recv, phase):
        return [
            remote(buffer.at[g], buffer.at[g], send.at[phase, k], recv.at[phase, g], peer_grp(k))
            for k in range(1, GROUPS)
        ]

    def wait_grp(buffer, send, recv, phase):
        for k in range(1, GROUPS):
            src = lax.rem(g + k, GROUPS)
            remote(
                buffer.at[src], buffer.at[src], send.at[phase, k], recv.at[phase, src], peer_grp(k)
            ).wait_recv()

    pending = []

    def launch(copies):
        for copy in copies:
            copy.start()
        pending.extend(copies)

    def coefficients(read, tiles, first_tile):
        total = jnp.zeros((2 * RHS, RANK), F32)
        for p in range(PER // 2):
            parts = []
            for side in range(2):
                leaf = 2 * p + side
                v = split2(read(leaf))
                field[PER + leaf] = v
                parts.append(fold(dot_nt(v, basis_high[leaf]) + dot_nt(v, basis_low[leaf])))
            tile = jnp.concatenate(parts, axis=1)
            tiles[first_tile + p] = tile
            c = split2(tile)
            for part in range(2):
                total += dot_nt(c, transfer2[part, :, 128 * p : 128 * (p + 1)])
        mid = fold(total)
        m = split2(mid)
        high, low = halves(mid_transfer[0])
        top = fold(dot_nt(m, high) + dot_nt(m, low))
        tiles[0] = jnp.concatenate([mid, top], axis=1)

    def column(leaf):
        return pl.ds(pl.multiple_of(leaf * LEAF, LEAF), LEAF)

    width, span = PER * LEAF, PACKED // 3
    halo1[1, :, 0:width] = start[...]
    for c in range(3):
        for r in range(8):
            halo1[1, r : r + 1, width + c * span : width + (c + 1) * span] = points[
                c : c + 1, r * span : (r + 1) * span
            ]
    for leaf in range(PER):
        high, low = halves(basis[leaf])
        basis_high[leaf] = high
        basis_low[leaf] = low
    for p in range(PER // 2):
        both = jnp.concatenate([transfer[2 * p], transfer[2 * p + 1]], axis=1)
        high, low = halves(both)
        transfer2[0, :, 128 * p : 128 * (p + 1)] = high
        transfer2[1, :, 128 * p : 128 * (p + 1)] = low
    pl.semaphore_wait(barrier, len(partners))
    launch(halo_copies(halo1, 0))

    own_gather = gather1.at[i]
    own_skel = []
    for p in range(PER // 2):
        tile = jnp.concatenate(
            [leaf_skel[:, 128 * p : 128 * (p + 1)], jnp.zeros((5, 128), F32)], axis=0
        )
        own_skel.append(tile)
        own_gather[2 + PER // 2 + p] = tile
    own_gather[1] = jnp.zeros((8, 128), F32)
    own_gather[1, 0:3, 0:RANK] = mid_skel[...]
    coefficients(lambda leaf: start[:, LEAF * leaf : LEAF * (leaf + 1)], own_gather, 2)
    launch(leaf_copies(gather1, coef_send, coef_recv, 0))

    centre = jnp.concatenate([jnp.floor(points[:, 0:1]), jnp.zeros((5, 1), F32)], axis=0)
    device = g * GSIZE + i
    base = device * PER

    def leaf_points(block, l):
        per_row = span // LEAF
        row, place = lax.div(l, per_row), lax.rem(l, per_row) * LEAF
        out = jnp.zeros((8, LEAF), F32)
        for c in range(3):
            cols = pl.ds(pl.multiple_of(width + c * span + place, LEAF), LEAF)
            out = jnp.where(rows_of((8, LEAF)) == c, halo1[block, pl.ds(row, 1), cols], out)
        return out

    def window_features(leaf, block, place):
        x = leaf_points(block, place) - centre
        wfeat[leaf] = source_pieces(source_rows(x)).T.astype(BF)
        return x

    def tangents(l):
        a = corners[base + PER + l] + 0x202020
        count = near_count[l]
        for s in range(NEAR):
            d = a - corners[base + near[l, s]]
            dx = (d & 255) - 32
            dy = ((d >> 8) & 255) - 32
            dz = (d >> 16) - 32
            d2 = jnp.minimum(dx * dx + dy * dy + dz * dz, 511)
            live = s < count
            tangent_a[l, s] = jnp.where(live, alphas[d2], 0.0)
            tangent_b[l, s] = jnp.where(live, betas[d2], 0.0)

    def own_features(n, carry):
        for t in range(4):
            l = 4 * n + t
            x = window_features(PER + l, 1, l)
            u = target_rows(x)
            urows[l] = u
            ufeat[l] = target_pieces(u).astype(BF)
            tangents(l)
        return carry

    lax.fori_loop(0, PER // 4, own_features, 0)
    for p in range(PER // 2):
        u = target_pieces(target_rows(own_skel[p] - centre))
        skel_feat[128 * p : 128 * (p + 1), :] = u.T.astype(BF)
    u = target_pieces(target_rows(own_gather[1] - centre))
    mid_feat[...] = u.T.astype(BF)
    for p in range(GROUPS // 2):
        top_tiles[p] = jnp.concatenate(
            [top_skel[:, 128 * p : 128 * (p + 1)], jnp.zeros((5, 128), F32)], axis=0
        )
    tile = top_tiles[lax.div(g, 2)]
    tile = jnp.where(lax.rem(g, 2) == 0, tile, pltpu.roll(tile, RANK, 1))
    top_feat[...] = target_pieces(target_rows(tile - centre)).T.astype(BF)

    def field_moments(first_leaf):
        lane8 = lax.broadcasted_iota(jnp.int32, (RHS, 8), 1)

        def some(n, carry):
            for t in range(8):
                leaf = first_leaf + 8 * n + t
                r = fold(dot(field[leaf], wfeat[leaf]))
                m = r[:, 0:8] + r[:, 8:16] + r[:, 32:40]
                moments[leaf, 0] = m
                moments[leaf, 1] = jnp.where(lane8 == 3, m[:, 4:5], 0.0)
            return carry

        lax.fori_loop(0, PER // 8, some, 0)

    field_moments(PER)
    for copy in halo_copies(halo1, 0):
        copy.wait_recv()

    def edge_features(n, carry):
        for t in range(4):
            l = 4 * n + t
            for block in (0, 2):
                leaf = block * PER + l
                window_features(leaf, block, l)
                field[leaf] = split2(halo1[block, :, column(l)])
        return carry

    lax.fori_loop(0, PER // 4, edge_features, 0)
    field_moments(0)
    field_moments(2 * PER)

    def evaluate(l):
        feat = ufeat[l]
        for c in range(0, LEAF, 64):
            for t in range(NEAR):
                q = dot(wfeat[near[l, t], c : c + 64, :], feat)
                r = kernel_value(q) - (q * tangent_b[l, t] + tangent_a[l, t])
                row = (l * NEAR + t) * LEAF + c
                remainder[pl.ds(pl.multiple_of(row, 64), 64), :] = r.astype(BF)

    def multiply(l):
        cols = []
        live = near_count[l]
        for t in range(NEAR):
            v = field[near[l, t]]
            cols.append(jnp.where(t < live, v, jnp.zeros_like(v)))
        row = pl.multiple_of(l * NEAR * LEAF, LEAF)
        near_acc[l] = dot(jnp.concatenate(cols, axis=1), remainder[pl.ds(row, NEAR * LEAF), :])

    def tangent_part(l):
        total = jnp.zeros((RHS, 8), F32)
        for s in range(NEAR):
            j = near[l, s]
            total += tangent_b[l, s] * moments[j, 0] + tangent_a[l, s] * moments[j, 1]
        out = total[:, 0:1] * urows[l, 0:1, :]
        for k in range(1, 5):
            out += total[:, k : k + 1] * urows[l, k : k + 1, :]
        return out

    remainder[(PER - 1) * NEAR * LEAF :, :] = jnp.zeros((NEAR * LEAF, LEAF), BF)

    def near_step(l, carry):
        multiply(lax.rem(l + PER - 1, PER))
        evaluate(l)
        return carry

    lax.fori_loop(0, PER // 2, near_step, 0)
    wait_leaf(gather1, coef_send, coef_recv, 0)
    for m in range(GSIZE):
        all1[g, m] = gather1[m, 0:2]
    launch(grp_copies(all1, all_send, all_recv, 0))
    lax.fori_loop(PER // 2, PER, near_step, 0)
    multiply(PER - 1)

    def moved(tile, index, want):
        return jnp.where((index & 1) == want, tile, pltpu.roll(tile, RANK, 1))

    def joined(first_tile, second_tile):
        return jnp.where(low_lanes, first_tile, second_tile)

    def far_tiles(feat, rows):
        return halves(kernel_value(dot(feat, source_pieces(rows).astype(BF))))

    def skeleton_rows(n, carry):
        for t in range(PER // 2):
            skel_rows[n * (PER // 2) + t] = source_rows(gather1[n, 2 + PER // 2 + t] - centre)
        return carry

    def far_matrix(lp, carry):
        for side in range(4):
            l = 4 * lp + side
            feat = skel_feat[pl.ds(pl.multiple_of(l * RANK, RANK), RANK), :]
            for p in range(FARL // 2):
                j1, j2 = far_leaf[l, 2 * p], far_leaf[l, 2 * p + 1]
                rows = joined(
                    moved(skel_rows[j1 >> 1], j1, 0), moved(skel_rows[j2 >> 1], j2, 1)
                )
                high, low = far_tiles(feat, rows)
                far_high[l, :, 128 * p : 128 * (p + 1)] = high
                far_low[l, :, 128 * p : 128 * (p + 1)] = low
        return carry

    def far_leaves(read):
        def some(n, carry):
            for q in range(2):
                lp = 2 * n + q
                parts = []
                for side in range(2):
                    l = 2 * lp + side
                    count = far_count[l]
                    cols = []
                    for p in range(FARL // 2):
                        s = 2 * p
                        j1, j2 = far_leaf[l, s], far_leaf[l, s + 1]
                        tile = joined(moved(read(j1), j1, 0), moved(read(j2), j2, 1))
                        slot = s + jnp.where(low_lanes, 0, 1)
                        cols.append(split2(jnp.where(slot < count, tile, 0.0)))
                    c = jnp.concatenate(cols, axis=1)
                    parts.append(dot_nt(far_high[l], c) + dot_nt(far_low[l], c))
                local[lp] = -FACTOR * fold(jnp.concatenate(parts, axis=0).T)
            return carry

        lax.fori_loop(0, PER // 4, some, 0)

    def upper_matrix(buffer):
        def read_mid(m):
            return source_rows(buffer[m >> 4, m & 15, 1] - centre)

        for p in range(FARM // 2):
            one, two = read_mid(far_mid[0, 2 * p]), read_mid(far_mid[0, 2 * p + 1])
            high, low = far_tiles(mid_feat[0:RANK, :], joined(one, pltpu.roll(two, RANK, 1)))
            mid_high[:, 128 * p : 128 * (p + 1)] = high
            mid_low[:, 128 * p : 128 * (p + 1)] = low

        def read_top(j, want):
            return moved(source_rows(top_tiles[j >> 1] - centre), j, want)

        for p in range(2):
            j1 = far_top[0, 2 * p]
            j2 = far_top[0, min(2 * p + 1, FART - 1)]
            high, low = far_tiles(top_feat[0:RANK, :], joined(read_top(j1, 0), read_top(j2, 1)))
            top_high[:, 128 * p : 128 * (p + 1)] = high
            top_low[:, 128 * p : 128 * (p + 1)] = low

    def upper_local(read):
        cols = []
        for p in range(FARM // 2):
            m1, m2 = far_mid[0, 2 * p], far_mid[0, 2 * p + 1]
            one, two = read(m1 >> 4, m1 & 15), read(m2 >> 4, m2 & 15)
            cols.append(split2(joined(one, pltpu.roll(two, RANK, 1))))
        c = jnp.concatenate(cols, axis=1)
        mid_far = -FACTOR * fold(dot_nt(c, mid_high[...]) + dot_nt(c, mid_low[...]))

        def top(j):
            total = read(j, 0)
            for m in range(1, GSIZE):
                total += read(j, m)
            return total

        t0, t1, t2 = (top(far_top[0, s]) for s in range(FART))
        cols = [
            split2(joined(pltpu.roll(t0, RANK, 1), t1)),
            split2(joined(pltpu.roll(t2, RANK, 1), jnp.zeros((RHS, 128), F32))),
        ]
        c = jnp.concatenate(cols, axis=1)
        top_far = -FACTOR * fold(dot_nt(c, top_high[...]) + dot_nt(c, top_low[...]))
        high, low = halves(mid_transfer[0])
        t = split2(top_far)
        return mid_far + fold(dot(t, high) + dot(t, low))

    def down(read_mid):
        m = split2(upper_local(read_mid))
        for p in range(PER // 2):
            down_part = sum(dot(m, transfer2[part, :, 128 * p : 128 * (p + 1)]) for part in range(2))
            local[p] += fold(down_part)

    def finish(n, store):
        for t in range(4):
            l = 4 * n + t
            tile = local[2 * n + t // 2]
            c = split2(tile[:, RANK * (t % 2) : RANK * (t % 2 + 1)])
            far = fold(dot(c, basis_high[l]) + dot(c, basis_low[l]))
            near_part = -FACTOR * (fold(near_acc[l]) + tangent_part(l))
            store(l, near_part + far)

    lax.fori_loop(0, GSIZE, skeleton_rows, 0)
    lax.fori_loop(0, PER // 4, far_matrix, 0)
    far_leaves(lambda j: gather1[j >> 4, 2 + ((j >> 1) & 7)])
    wait_grp(all1, all_send, all_recv, 0)
    upper_matrix(all1)
    noise_value = noise[0]

    def first_leaves(n, carry):
        def store(l, value):
            cols = column(l)
            r = rhs[:, cols] - (noise_value * start[:, cols] + value)
            first[:, cols] = r
            halo2[1, :, cols] = r

        finish(n, store)
        return carry

    left, right = (slice(None), slice(0, width // 2)), (slice(None), slice(width // 2, width))
    down(lambda a, b: all1[a, b, 0])
    lax.fori_loop(0, PER // 8, first_leaves, 0)
    launch(halo_copies(halo2, 1, *left))
    lax.fori_loop(PER // 8, PER // 4, first_leaves, 0)
    launch(halo_copies(halo2, 2, *right))

    coefficients(lambda leaf: first[:, LEAF * leaf : LEAF * (leaf + 1)], gather2.at[i], 1)
    launch(leaf_copies(gather2, coef_send, coef_recv, 1))
    field_moments(PER)
    for copy in halo_copies(halo2, 1, *left) + halo_copies(halo2, 2, *right):
        copy.wait_recv()

    def edge_fields(n, carry):
        for t in range(4):
            l = 4 * n + t
            for block in (0, 2):
                field[block * PER + l] = split2(halo2[block, :, column(l)])
        return carry

    lax.fori_loop(0, PER // 4, edge_fields, 0)
    field_moments(0)
    field_moments(2 * PER)

    def near_again(l, carry):
        multiply(l)
        return carry

    lax.fori_loop(0, PER // 2, near_again, 0)
    wait_leaf(gather2, coef_send, coef_recv, 1)
    for m in range(GSIZE):
        all2[g, m] = gather2[m, 0]
    launch(grp_copies(all2, all_send, all_recv, 1))
    lax.fori_loop(PER // 2, PER, near_again, 0)
    far_leaves(lambda j: gather2[j >> 4, 1 + ((j >> 1) & 7)])
    wait_grp(all2, all_send, all_recv, 1)

    def image_leaves(n, carry):
        def store(l, value):
            cols = column(l)
            image[:, cols] = noise_value * first[:, cols] + value

        finish(n, store)
        return carry

    down(lambda a, b: all2[a, b])
    lax.fori_loop(0, PER // 4, image_leaves, 0)

    dots = jnp.zeros((RHS, LEAF), F32)
    squares = jnp.zeros((RHS, LEAF), F32)
    for l in range(PER):
        cols = slice(LEAF * l, LEAF * (l + 1))
        y = image[:, cols]
        dots += first[:, cols] * y
        squares += y * y
    sums1[i] = jnp.where(
        low_lanes,
        jnp.sum(dots, axis=1, keepdims=True),
        jnp.sum(squares, axis=1, keepdims=True),
    )
    launch(leaf_copies(sums1, sum_send, sum_recv, 0))
    wait_leaf(sums1, sum_send, sum_recv, 0)
    total = sums1[0]
    for k in range(1, GSIZE):
        total += sums1[k]
    sums2[g] = total
    launch(grp_copies(sums2, tot_send, tot_recv, 0))
    wait_grp(sums2, tot_send, tot_recv, 0)
    total = sums2[0]
    for k in range(1, GROUPS):
        total += sums2[k]
    total = total / (LEAVES * LEAF)
    alpha = total[:, 0:1] / (total[:, RANK : RANK + 1] + 1e-6)
    step[...] = jnp.broadcast_to(alpha, (RHS, 128))
    for copy in pending:
        copy.wait_send()


def shards(*args):
    smem = pl.BlockSpec(memory_space=pltpu.SMEM)
    vmem = pl.BlockSpec(memory_space=pltpu.VMEM)
    alphas, betas = tangent_tables()
    tables = (jnp.asarray(morton_table()), jnp.asarray(alphas), jnp.asarray(betas))
    out = jax.ShapeDtypeStruct((RHS, PER * LEAF), F32)
    tile = (8, 128)

    def buffer(shape, dtype=F32):
        return pltpu.VMEM(shape, dtype)

    def sems(*shape):
        return pltpu.SemaphoreType.DMA(shape)

    scratch = [
        buffer((PER * NEAR * LEAF, LEAF), BF),
        buffer((PER, RANK, FARL * RANK), BF),
        buffer((PER, RANK, FARL * RANK), BF),
        buffer((RANK, FARM * RANK), BF),
        buffer((RANK, FARM * RANK), BF),
        buffer((RANK, 4 * RANK), BF),
        buffer((RANK, 4 * RANK), BF),
        buffer((3, 8, PER * LEAF + PACKED)),
        buffer((3, 8, PER * LEAF)),
        buffer((GSIZE, TILES1) + tile),
        buffer((GSIZE, TILES2) + tile),
        buffer((GROUPS, GSIZE, 2) + tile),
        buffer((GROUPS, GSIZE) + tile),
        buffer((GSIZE,) + tile),
        buffer((GROUPS,) + tile),
        buffer((WIN, 2 * RHS, LEAF), BF),
        buffer((WIN, LEAF, PIECES), BF),
        buffer((PER, PIECES, LEAF), BF),
        buffer((PER, 8, LEAF)),
        buffer((WIN, 2, RHS, 8)),
        buffer((GSIZE * PER // 2,) + tile),
        pltpu.SMEM((PER, NEAR), F32),
        pltpu.SMEM((PER, NEAR), F32),
        buffer((PER * RANK, PIECES), BF),
        buffer((128, PIECES), BF),
        buffer((128, PIECES), BF),
        buffer((GROUPS // 2,) + tile),
        buffer((PER, RANK, LEAF), BF),
        buffer((PER, RANK, LEAF), BF),
        buffer((2, RANK, PER * RANK), BF),
        buffer((PER, 2 * RHS, LEAF)),
        buffer((PER // 2,) + tile),
        sems(3, 2),
        sems(3, 2),
        sems(2, GSIZE),
        sems(2, GSIZE),
        sems(2, GROUPS),
        sems(2, GROUPS),
        sems(1, GSIZE),
        sems(1, GSIZE),
        sems(1, GROUPS),
        sems(1, GROUPS),
    ]
    first, image, step = pl.pallas_call(
        body,
        out_shape=(out, out, jax.ShapeDtypeStruct(tile, F32)),
        in_specs=[vmem] * 9 + [smem] * 10,
        out_specs=(vmem, vmem, vmem),
        scratch_shapes=scratch,
        compiler_params=pltpu.CompilerParams(
            collective_id=0, has_side_effects=True, vmem_limit_bytes=61 << 20
        ),
    )(*args, *tables)
    alpha = step[:, 0:1]
    return args[2] + alpha * first, first - alpha * image


def solution(mesh):
    columns = P(None, ("grp", "leaf"))
    blocks = P(("grp", "leaf"), None, None)
    lists = P(("grp", "leaf"), None)
    return jax.shard_map(
        shards,
        mesh=mesh,
        in_specs=(
            columns,
            columns,
            columns,
            columns,
            columns,
            P(),
            blocks,
            blocks,
            blocks,
            P(),
            lists,
            P(("grp", "leaf")),
            lists,
            P(("grp", "leaf")),
            lists,
            P("grp", None),
        ),
        out_specs=(columns, columns),
        check_vma=False,
    )
```

```python
import functools
import math

import jax
import jax.numpy as jnp
import numpy as np
from jax import lax
from jax.experimental import pallas as pl
from jax.experimental.pallas import tpu as pltpu
from jax.sharding import PartitionSpec as P

BF = jnp.bfloat16
F32 = jnp.float32
MESH = pl.DeviceIdType.MESH
NT = (((1,), (1,)), ((), ()))

LEAF = 256
RANK = 64
RHS = 8
PER = 16
NEAR = 16
FARL = 32
FARM = 16
FART = 3
GROUPS = 8
GSIZE = 16
LEAVES = 2048
WIN = 3 * PER
PIECES = 48
TILES1 = 2 + PER
TILES2 = 1 + PER // 2
PACKED = 3 * PER * LEAF // 8

LOG2E = math.log2(math.e)
KAPPA = 0.75 * LOG2E * LOG2E
FACTOR = math.e * math.log(2.0)
TINY = 1e-30


def morton_table():
    ids = np.arange(LEAVES)
    coords = [np.zeros_like(ids) for _ in range(3)]
    for bit in range(30):
        coords[bit % 3] += ((ids >> bit) & 1) << (bit // 3)
    packed = coords[0] + 256 * coords[1] + 65536 * coords[2]
    return np.pad(packed, (PER, PER)).astype(np.int32)


def tangent_tables():
    mean = 0.75 * (np.arange(512) + 0.5)
    s = np.sqrt(mean)
    beta = 0.5 * np.exp(-s) / (LOG2E * LOG2E) / FACTOR
    alpha = -(1 + s) * np.exp(-s) / FACTOR - beta * mean * LOG2E * LOG2E
    alpha = np.append(alpha, -LOG2E)
    return alpha.astype(np.float32), beta.astype(np.float32)


def rounded(x):
    return x.astype(BF).astype(F32)


def split2(x):
    high = rounded(x)
    return jnp.concatenate([high, x - high], axis=0).astype(BF)


def split3(x):
    first = rounded(x)
    rest = x - first
    second = rounded(rest)
    return first, second, rounded(rest - second)


def source_pieces(w):
    a, b, c = split3(w)
    return jnp.concatenate([a, b, a, b, c, a], axis=0)


def target_pieces(u):
    a, b, c = split3(u)
    return jnp.concatenate([a, a, b, b, a, c], axis=0)


def rows_of(shape):
    return lax.broadcasted_iota(jnp.int32, shape, 0)


def source_rows(x):
    row = rows_of(x.shape)
    x = jnp.where(row < 3, x, 0.0)
    norm = KAPPA * jnp.sum(x * x, axis=0, keepdims=True)
    return jnp.where(row == 3, norm, jnp.where(row == 4, 1.0, x))


def target_rows(x):
    row = rows_of(x.shape)
    x = jnp.where(row < 3, x, 0.0)
    norm = KAPPA * jnp.sum(x * x, axis=0, keepdims=True)
    return jnp.where(row == 4, norm, jnp.where(row == 3, 1.0, (-2.0 * KAPPA) * x))


def kernel_value(q, shift):
    y = shift - q * lax.rsqrt(q)
    return y * jnp.exp2(y)


def halves(x):
    high = x.astype(BF)
    return high, (x - high.astype(F32)).astype(BF)


def dot(a, b):
    return jnp.dot(a, b, preferred_element_type=F32)


def dot_nt(a, b):
    return lax.dot_general(a, b, NT, preferred_element_type=F32)


def fold(x):
    return x[:RHS] + x[RHS:]


def body(
    points,
    rhs,
    start,
    leaf_skel,
    mid_skel,
    top_skel,
    basis,
    transfer,
    mid_transfer,
    noise,
    near,
    near_count,
    far_leaf,
    far_count,
    far_mid,
    far_top,
    corners,
    alphas,
    betas,
    first,
    image,
    step,
    remainder0,
    remainder1,
    far_high,
    far_low,
    mid_high,
    mid_low,
    top_high,
    top_low,
    halo1,
    halo2,
    gather1,
    gather2,
    all1,
    all2,
    sums1,
    sums2,
    field,
    wfeat,
    ufeat,
    urows,
    moments,
    skel_rows,
    tangent_a,
    tangent_b,
    skel_feat,
    mid_feat,
    top_feat,
    top_tiles,
    basis_high,
    basis_low,
    transfer2,
    near_acc,
    local,
    halo_send,
    halo_recv,
    coef_send,
    coef_recv,
    all_send,
    all_recv,
    sum_send,
    sum_recv,
    tot_send,
    tot_recv,
):
    g = lax.axis_index("grp")
    i = lax.axis_index("leaf")
    lane = lax.broadcasted_iota(jnp.int32, (RHS, 128), 1)
    low_lanes = lane < RANK
    tile_shape = (RHS, 128)

    def peer_leaf(k):
        return (g, lax.rem(i + k, GSIZE))

    def peer_grp(k):
        return (lax.rem(g + k, GROUPS), i)

    up = i + 1
    down = i + GSIZE - 1
    after = (lax.rem(g + lax.div(up, GSIZE), GROUPS), lax.rem(up, GSIZE))
    before = (lax.rem(g + GROUPS - 1 + lax.div(down, GSIZE), GROUPS), lax.rem(down, GSIZE))

    barrier = pltpu.get_barrier_semaphore()
    partners = (
        [peer_leaf(k) for k in range(1, GSIZE)]
        + [peer_grp(k) for k in range(1, GROUPS)]
        + [after, before]
    )
    for partner in partners:
        pl.semaphore_signal(barrier, inc=1, device_id=partner, device_id_type=MESH)

    def remote(src, dst, send, recv, device):
        return pltpu.make_async_remote_copy(
            src_ref=src,
            dst_ref=dst,
            send_sem=send,
            recv_sem=recv,
            device_id=device,
            device_id_type=MESH,
        )

    def halo_copies(window, phase, *where):
        own, low, high = (window.at[(block,) + where] for block in (1, 0, 2))
        return [
            remote(own, low, halo_send.at[phase, 0], halo_recv.at[phase, 0], after),
            remote(own, high, halo_send.at[phase, 1], halo_recv.at[phase, 1], before),
        ]

    def leaf_copies(buffer, send, recv, phase):
        own = buffer.at[i]
        return [
            remote(own, own, send.at[phase, k], recv.at[phase, i], peer_leaf(k))
            for k in range(1, GSIZE)
        ]

    def wait_leaf(buffer, send, recv, phase):
        for k in range(1, GSIZE):
            src = lax.rem(i + k, GSIZE)
            theirs = buffer.at[src]
            remote(theirs, theirs, send.at[phase, k], recv.at[phase, src], peer_leaf(k)).wait_recv()

    def grp_copies(buffer, send, recv, phase):
        return [
            remote(buffer.at[g], buffer.at[g], send.at[phase, k], recv.at[phase, g], peer_grp(k))
            for k in range(1, GROUPS)
        ]

    def wait_grp(buffer, send, recv, phase):
        for k in range(1, GROUPS):
            src = lax.rem(g + k, GROUPS)
            remote(
                buffer.at[src], buffer.at[src], send.at[phase, k], recv.at[phase, src], peer_grp(k)
            ).wait_recv()

    pending = []

    def launch(copies):
        for copy in copies:
            copy.start()
        pending.extend(copies)

    def coefficients(read, tiles, first_tile):
        total = jnp.zeros((2 * RHS, RANK), F32)
        for p in range(PER // 2):
            parts = []
            for side in range(2):
                leaf = 2 * p + side
                v = split2(read(leaf))
                field[PER + leaf] = v
                parts.append(fold(dot_nt(v, basis_high[leaf]) + dot_nt(v, basis_low[leaf])))
            tile = jnp.concatenate(parts, axis=1)
            tiles[first_tile + p] = tile
            c = split2(tile)
            for part in range(2):
                total += dot_nt(c, transfer2[part, :, 128 * p : 128 * (p + 1)])
        mid = fold(total)
        m = split2(mid)
        high, low = halves(mid_transfer[0])
        top = fold(dot_nt(m, high) + dot_nt(m, low))
        tiles[0] = jnp.concatenate([mid, top], axis=1)

    def column(leaf):
        return pl.ds(pl.multiple_of(leaf * LEAF, LEAF), LEAF)

    width, span = PER * LEAF, PACKED // 3
    halo1[1, :, 0:width] = start[...]
    for c in range(3):
        for r in range(8):
            halo1[1, r : r + 1, width + c * span : width + (c + 1) * span] = points[
                c : c + 1, r * span : (r + 1) * span
            ]
    for leaf in range(PER):
        high, low = halves(basis[leaf])
        basis_high[leaf] = high
        basis_low[leaf] = low
    for p in range(PER // 2):
        both = jnp.concatenate([transfer[2 * p], transfer[2 * p + 1]], axis=1)
        high, low = halves(both)
        transfer2[0, :, 128 * p : 128 * (p + 1)] = high
        transfer2[1, :, 128 * p : 128 * (p + 1)] = low
    pl.semaphore_wait(barrier, len(partners))
    launch(halo_copies(halo1, 0))

    own_gather = gather1.at[i]
    own_skel = []
    for p in range(PER // 2):
        tile = jnp.concatenate(
            [leaf_skel[:, 128 * p : 128 * (p + 1)], jnp.zeros((5, 128), F32)], axis=0
        )
        own_skel.append(tile)
        own_gather[2 + PER // 2 + p] = tile
    own_gather[1] = jnp.zeros((8, 128), F32)
    own_gather[1, 0:3, 0:RANK] = mid_skel[...]
    coefficients(lambda leaf: start[:, LEAF * leaf : LEAF * (leaf + 1)], own_gather, 2)
    launch(leaf_copies(gather1, coef_send, coef_recv, 0))

    centre = jnp.concatenate([jnp.floor(points[:, 0:1]), jnp.zeros((5, 1), F32)], axis=0)
    device = g * GSIZE + i
    base = device * PER

    def leaf_points(block, l):
        per_row = span // LEAF
        row, place = lax.div(l, per_row), lax.rem(l, per_row) * LEAF
        out = jnp.zeros((8, LEAF), F32)
        for c in range(3):
            cols = pl.ds(pl.multiple_of(width + c * span + place, LEAF), LEAF)
            out = jnp.where(rows_of((8, LEAF)) == c, halo1[block, pl.ds(row, 1), cols], out)
        return out

    def window_features(leaf, block, place):
        x = leaf_points(block, place) - centre
        wfeat[leaf] = source_pieces(source_rows(x)).T.astype(BF)
        return x

    def tangents(l):
        a = corners[base + PER + l] + 0x202020
        count = near_count[l]
        for s in range(NEAR):
            d = a - corners[base + near[l, s]]
            dx = (d & 255) - 32
            dy = ((d >> 8) & 255) - 32
            dz = (d >> 16) - 32
            d2 = jnp.minimum(dx * dx + dy * dy + dz * dz, 511)
            live = s < count
            tangent_a[l, s] = jnp.where(live, alphas[d2], 0.0)
            tangent_b[l, s] = jnp.where(live, betas[d2], 0.0)

    def own_features(n, carry):
        for t in range(4):
            l = 4 * n + t
            x = window_features(PER + l, 1, l)
            u = target_rows(x)
            urows[l] = u
            ufeat[l] = target_pieces(u).astype(BF)
            tangents(l)
        return carry

    lax.fori_loop(0, PER // 4, own_features, 0)
    for p in range(PER // 2):
        u = target_pieces(target_rows(own_skel[p] - centre))
        skel_feat[128 * p : 128 * (p + 1), :] = u.T.astype(BF)
    u = target_pieces(target_rows(own_gather[1] - centre))
    mid_feat[...] = u.T.astype(BF)
    for p in range(GROUPS // 2):
        top_tiles[p] = jnp.concatenate(
            [top_skel[:, 128 * p : 128 * (p + 1)], jnp.zeros((5, 128), F32)], axis=0
        )
    tile = top_tiles[lax.div(g, 2)]
    tile = jnp.where(lax.rem(g, 2) == 0, tile, pltpu.roll(tile, RANK, 1))
    top_feat[...] = target_pieces(target_rows(tile - centre)).T.astype(BF)

    def field_moments(first_leaf):
        lane8 = lax.broadcasted_iota(jnp.int32, (RHS, 8), 1)

        def some(n, carry):
            for t in range(8):
                leaf = first_leaf + 8 * n + t
                r = fold(dot(field[leaf], wfeat[leaf]))
                m = r[:, 0:8] + r[:, 8:16] + r[:, 32:40]
                moments[leaf, 0] = m
                moments[leaf, 1] = jnp.where(lane8 == 3, m[:, 4:5], 0.0)
            return carry

        lax.fori_loop(0, PER // 8, some, 0)

    field_moments(PER)
    for copy in halo_copies(halo1, 0):
        copy.wait_recv()

    def edge_features(n, carry):
        for t in range(4):
            l = 4 * n + t
            for block in (0, 2):
                leaf = block * PER + l
                window_features(leaf, block, l)
                field[leaf] = split2(halo1[block, :, column(l)])
        return carry

    lax.fori_loop(0, PER // 4, edge_features, 0)
    field_moments(0)
    field_moments(2 * PER)

    shift = alphas[512]
    remainders = (remainder0, remainder1)

    def evaluate(n, side):
        l = 2 * n + side
        feat = ufeat[l]
        for c in range(0, LEAF, 64):
            for t in range(NEAR):
                q = jnp.maximum(dot(wfeat[near[l, t], c : c + 64, :], feat), TINY)
                r = kernel_value(q, shift) - (q * tangent_b[l, t] + tangent_a[l, t])
                row = (n * NEAR + t) * LEAF + c
                remainders[side][pl.ds(pl.multiple_of(row, 64), 64), :] = r.astype(BF)

    def multiply(n, side):
        l = 2 * n + side
        cols = []
        live = near_count[l]
        for t in range(NEAR):
            v = field[near[l, t]]
            cols.append(jnp.where(t < live, v, jnp.zeros_like(v)))
        rows = pl.ds(pl.multiple_of(n * NEAR * LEAF, LEAF), NEAR * LEAF)
        near_acc[l] = dot(jnp.concatenate(cols, axis=1), remainders[side][rows, :])

    def tangent_part(l):
        total = jnp.zeros((RHS, 8), F32)
        for s in range(NEAR):
            j = near[l, s]
            total += tangent_b[l, s] * moments[j, 0] + tangent_a[l, s] * moments[j, 1]
        out = total[:, 0:1] * urows[l, 0:1, :]
        for k in range(1, 5):
            out += total[:, k : k + 1] * urows[l, k : k + 1, :]
        return out

    remainder1[(PER // 2 - 1) * NEAR * LEAF :, :] = jnp.zeros((NEAR * LEAF, LEAF), BF)

    def near_step(n, carry):
        multiply(lax.rem(n + PER // 2 - 1, PER // 2), 1)
        evaluate(n, 0)
        multiply(n, 0)
        evaluate(n, 1)
        return carry

    lax.fori_loop(0, PER // 4, near_step, 0)
    wait_leaf(gather1, coef_send, coef_recv, 0)
    for m in range(GSIZE):
        all1[g, m] = gather1[m, 0:2]
    launch(grp_copies(all1, all_send, all_recv, 0))
    lax.fori_loop(PER // 4, PER // 2, near_step, 0)
    multiply(PER // 2 - 1, 1)

    def moved(tile, index, want):
        return jnp.where((index & 1) == want, tile, pltpu.roll(tile, RANK, 1))

    def joined(first_tile, second_tile):
        return jnp.where(low_lanes, first_tile, second_tile)

    def far_tiles(feat, rows):
        q = jnp.maximum(dot(feat, source_pieces(rows).astype(BF)), TINY)
        return halves(kernel_value(q, shift))

    def skeleton_rows(n, carry):
        for t in range(PER // 2):
            skel_rows[n * (PER // 2) + t] = source_rows(gather1[n, 2 + PER // 2 + t] - centre)
        return carry

    def far_matrix(lp, carry):
        for side in range(4):
            l = 4 * lp + side
            feat = skel_feat[pl.ds(pl.multiple_of(l * RANK, RANK), RANK), :]
            for p in range(FARL // 2):
                j1, j2 = far_leaf[l, 2 * p], far_leaf[l, 2 * p + 1]
                rows = joined(
                    moved(skel_rows[j1 >> 1], j1, 0), moved(skel_rows[j2 >> 1], j2, 1)
                )
                high, low = far_tiles(feat, rows)
                far_high[l, :, 128 * p : 128 * (p + 1)] = high
                far_low[l, :, 128 * p : 128 * (p + 1)] = low
        return carry

    def far_leaves(read):
        def some(n, carry):
            for q in range(2):
                lp = 2 * n + q
                parts = []
                for side in range(2):
                    l = 2 * lp + side
                    count = far_count[l]
                    cols = []
                    for p in range(FARL // 2):
                        s = 2 * p
                        j1, j2 = far_leaf[l, s], far_leaf[l, s + 1]
                        tile = joined(moved(read(j1), j1, 0), moved(read(j2), j2, 1))
                        slot = s + jnp.where(low_lanes, 0, 1)
                        cols.append(split2(jnp.where(slot < count, tile, 0.0)))
                    c = jnp.concatenate(cols, axis=1)
                    parts.append(dot_nt(far_high[l], c) + dot_nt(far_low[l], c))
                local[lp] = -FACTOR * fold(jnp.concatenate(parts, axis=0).T)
            return carry

        lax.fori_loop(0, PER // 4, some, 0)

    def upper_matrix(buffer):
        def read_mid(m):
            return source_rows(buffer[m >> 4, m & 15, 1] - centre)

        for p in range(FARM // 2):
            one, two = read_mid(far_mid[0, 2 * p]), read_mid(far_mid[0, 2 * p + 1])
            high, low = far_tiles(mid_feat[0:RANK, :], joined(one, pltpu.roll(two, RANK, 1)))
            mid_high[:, 128 * p : 128 * (p + 1)] = high
            mid_low[:, 128 * p : 128 * (p + 1)] = low

        def read_top(j, want):
            return moved(source_rows(top_tiles[j >> 1] - centre), j, want)

        for p in range(2):
            j1 = far_top[0, 2 * p]
            j2 = far_top[0, min(2 * p + 1, FART - 1)]
            high, low = far_tiles(top_feat[0:RANK, :], joined(read_top(j1, 0), read_top(j2, 1)))
            top_high[:, 128 * p : 128 * (p + 1)] = high
            top_low[:, 128 * p : 128 * (p + 1)] = low

    def upper_local(read, read_top):
        cols = []
        for p in range(FARM // 2):
            m1, m2 = far_mid[0, 2 * p], far_mid[0, 2 * p + 1]
            cols.append(split2(joined(read(m1, 0), read(m2, 1))))
        c = jnp.concatenate(cols, axis=1)
        mid_far = -FACTOR * fold(dot_nt(c, mid_high[...]) + dot_nt(c, mid_low[...]))

        t0, t1, t2 = (read_top(far_top[0, s]) for s in range(FART))
        cols = [
            split2(joined(pltpu.roll(t0, RANK, 1), t1)),
            split2(joined(pltpu.roll(t2, RANK, 1), jnp.zeros((RHS, 128), F32))),
        ]
        c = jnp.concatenate(cols, axis=1)
        top_far = -FACTOR * fold(dot_nt(c, top_high[...]) + dot_nt(c, top_low[...]))
        high, low = halves(mid_transfer[0])
        t = split2(top_far)
        return mid_far + fold(dot(t, high) + dot(t, low))

    def down(read_mid, read_top):
        m = split2(upper_local(read_mid, read_top))
        for p in range(PER // 2):
            down_part = sum(dot(m, transfer2[part, :, 128 * p : 128 * (p + 1)]) for part in range(2))
            local[p] += fold(down_part)

    def finish(n, store):
        for t in range(4):
            l = 4 * n + t
            tile = local[2 * n + t // 2]
            c = split2(tile[:, RANK * (t % 2) : RANK * (t % 2 + 1)])
            far = fold(dot(c, basis_high[l]) + dot(c, basis_low[l]))
            near_part = -FACTOR * (fold(near_acc[l]) + tangent_part(l))
            store(l, near_part + far)

    lax.fori_loop(0, GSIZE, skeleton_rows, 0)
    lax.fori_loop(0, PER // 4, far_matrix, 0)
    far_leaves(lambda j: gather1[j >> 4, 2 + ((j >> 1) & 7)])
    wait_grp(all1, all_send, all_recv, 0)
    upper_matrix(all1)
    noise_value = noise[0]

    def first_leaves(n, carry):
        def store(l, value):
            cols = column(l)
            r = rhs[:, cols] - (noise_value * start[:, cols] + value)
            first[:, cols] = r
            halo2[1, :, cols] = r

        finish(n, store)
        return carry

    left, right = (slice(None), slice(0, width // 2)), (slice(None), slice(width // 2, width))
    def mid1(m, want):
        tile = all1[m >> 4, m & 15, 0]
        return pltpu.roll(tile, RANK, 1) if want else tile

    def top1(j):
        total = all1[j, 0, 0]
        for m in range(1, GSIZE):
            total += all1[j, m, 0]
        return total

    down(mid1, top1)
    lax.fori_loop(0, PER // 8, first_leaves, 0)
    launch(halo_copies(halo2, 1, *left))
    lax.fori_loop(PER // 8, PER // 4, first_leaves, 0)
    launch(halo_copies(halo2, 2, *right))

    coefficients(lambda leaf: first[:, LEAF * leaf : LEAF * (leaf + 1)], gather2.at[i], 1)
    launch(leaf_copies(gather2, coef_send, coef_recv, 1))
    field_moments(PER)
    for copy in halo_copies(halo2, 1, *left) + halo_copies(halo2, 2, *right):
        copy.wait_recv()

    def edge_fields(n, carry):
        for t in range(4):
            l = 4 * n + t
            for block in (0, 2):
                field[block * PER + l] = split2(halo2[block, :, column(l)])
        return carry

    lax.fori_loop(0, PER // 4, edge_fields, 0)
    field_moments(0)
    field_moments(2 * PER)

    def near_again(n, carry):
        multiply(n, 0)
        multiply(n, 1)
        return carry

    lax.fori_loop(0, PER // 2 - 2, near_again, 0)
    wait_leaf(gather2, coef_send, coef_recv, 1)
    group_top = jnp.zeros(tile_shape, F32)
    for p in range(GSIZE // 2):
        one, two = gather2[2 * p, 0], gather2[2 * p + 1, 0]
        all2[g, p] = joined(one, pltpu.roll(two, RANK, 1))
        group_top += one + two
    all2[g, GSIZE // 2] = group_top
    launch(grp_copies(all2, all_send, all_recv, 1))
    lax.fori_loop(PER // 2 - 2, PER // 2, near_again, 0)
    far_leaves(lambda j: gather2[j >> 4, 1 + ((j >> 1) & 7)])
    wait_grp(all2, all_send, all_recv, 1)

    def image_leaves(n, carry):
        def store(l, value):
            cols = column(l)
            image[:, cols] = noise_value * first[:, cols] + value

        finish(n, store)
        return carry

    down(
        lambda m, want: moved(all2[m >> 4, (m & 15) >> 1], m, want),
        lambda j: all2[j, GSIZE // 2],
    )
    lax.fori_loop(0, PER // 4, image_leaves, 0)

    dots = jnp.zeros((RHS, LEAF), F32)
    squares = jnp.zeros((RHS, LEAF), F32)
    for l in range(PER):
        cols = slice(LEAF * l, LEAF * (l + 1))
        y = image[:, cols]
        dots += first[:, cols] * y
        squares += y * y
    sums1[i] = jnp.where(
        low_lanes,
        jnp.sum(dots, axis=1, keepdims=True),
        jnp.sum(squares, axis=1, keepdims=True),
    )
    launch(leaf_copies(sums1, sum_send, sum_recv, 0))
    wait_leaf(sums1, sum_send, sum_recv, 0)
    total = sums1[0]
    for k in range(1, GSIZE):
        total += sums1[k]
    sums2[g] = total
    launch(grp_copies(sums2, tot_send, tot_recv, 0))
    wait_grp(sums2, tot_send, tot_recv, 0)
    total = sums2[0]
    for k in range(1, GROUPS):
        total += sums2[k]
    total = total / (LEAVES * LEAF)
    alpha = total[:, 0:1] / (total[:, RANK : RANK + 1] + 1e-6)
    step[...] = jnp.broadcast_to(alpha, (RHS, 128))
    for copy in pending:
        copy.wait_send()


def shards(*args):
    smem = pl.BlockSpec(memory_space=pltpu.SMEM)
    vmem = pl.BlockSpec(memory_space=pltpu.VMEM)
    alphas, betas = tangent_tables()
    tables = (jnp.asarray(morton_table()), jnp.asarray(alphas), jnp.asarray(betas))
    out = jax.ShapeDtypeStruct((RHS, PER * LEAF), F32)
    tile = (8, 128)

    def buffer(shape, dtype=F32):
        return pltpu.VMEM(shape, dtype)

    def sems(*shape):
        return pltpu.SemaphoreType.DMA(shape)

    scratch = [
        buffer((PER // 2 * NEAR * LEAF, LEAF), BF),
        buffer((PER // 2 * NEAR * LEAF, LEAF), BF),
        buffer((PER, RANK, FARL * RANK), BF),
        buffer((PER, RANK, FARL * RANK), BF),
        buffer((RANK, FARM * RANK), BF),
        buffer((RANK, FARM * RANK), BF),
        buffer((RANK, 4 * RANK), BF),
        buffer((RANK, 4 * RANK), BF),
        buffer((3, 8, PER * LEAF + PACKED)),
        buffer((3, 8, PER * LEAF)),
        buffer((GSIZE, TILES1) + tile),
        buffer((GSIZE, TILES2) + tile),
        buffer((GROUPS, GSIZE, 2) + tile),
        buffer((GROUPS, GSIZE // 2 + 1) + tile),
        buffer((GSIZE,) + tile),
        buffer((GROUPS,) + tile),
        buffer((WIN, 2 * RHS, LEAF), BF),
        buffer((WIN, LEAF, PIECES), BF),
        buffer((PER, PIECES, LEAF), BF),
        buffer((PER, 8, LEAF)),
        buffer((WIN, 2, RHS, 8)),
        buffer((GSIZE * PER // 2,) + tile),
        pltpu.SMEM((PER, NEAR), F32),
        pltpu.SMEM((PER, NEAR), F32),
        buffer((PER * RANK, PIECES), BF),
        buffer((128, PIECES), BF),
        buffer((128, PIECES), BF),
        buffer((GROUPS // 2,) + tile),
        buffer((PER, RANK, LEAF), BF),
        buffer((PER, RANK, LEAF), BF),
        buffer((2, RANK, PER * RANK), BF),
        buffer((PER, 2 * RHS, LEAF)),
        buffer((PER // 2,) + tile),
        sems(3, 2),
        sems(3, 2),
        sems(2, GSIZE),
        sems(2, GSIZE),
        sems(2, GROUPS),
        sems(2, GROUPS),
        sems(1, GSIZE),
        sems(1, GSIZE),
        sems(1, GROUPS),
        sems(1, GROUPS),
    ]
    first, image, step = pl.pallas_call(
        body,
        out_shape=(out, out, jax.ShapeDtypeStruct(tile, F32)),
        in_specs=[vmem] * 9 + [smem] * 10,
        out_specs=(vmem, vmem, vmem),
        scratch_shapes=scratch,
        compiler_params=pltpu.CompilerParams(
            collective_id=0, has_side_effects=True, vmem_limit_bytes=61 << 20
        ),
    )(*args, *tables)
    alpha = step[:, 0:1]
    return args[2] + alpha * first, first - alpha * image


def solution(mesh):
    columns = P(None, ("grp", "leaf"))
    blocks = P(("grp", "leaf"), None, None)
    lists = P(("grp", "leaf"), None)
    return jax.shard_map(
        shards,
        mesh=mesh,
        in_specs=(
            columns,
            columns,
            columns,
            columns,
            columns,
            P(),
            blocks,
            blocks,
            blocks,
            P(),
            lists,
            P(("grp", "leaf")),
            lists,
            P(("grp", "leaf")),
            lists,
            P("grp", None),
        ),
        out_specs=(columns, columns),
        check_vma=False,
    )
```

```python
import functools
import math

import jax
import jax.numpy as jnp
import numpy as np
from jax import lax
from jax.experimental import pallas as pl
from jax.experimental.pallas import tpu as pltpu
from jax.sharding import PartitionSpec as P

BF = jnp.bfloat16
F32 = jnp.float32
MESH = pl.DeviceIdType.MESH
NT = (((1,), (1,)), ((), ()))

LEAF = 256
RANK = 64
RHS = 8
PER = 16
NEAR = 16
FARL = 32
FARM = 16
FART = 3
GROUPS = 8
GSIZE = 16
LEAVES = 2048
WIN = 3 * PER
PIECES = 48
TILES1 = 5 + PER // 2
TILES2 = PER // 2
PACKED = 3 * PER * LEAF // 8

LOG2E = math.log2(math.e)
KAPPA = 0.75 * LOG2E * LOG2E
FACTOR = math.e * math.log(2.0)
TINY = 1e-30


def morton_table():
    ids = np.arange(LEAVES)
    coords = [np.zeros_like(ids) for _ in range(3)]
    for bit in range(30):
        coords[bit % 3] += ((ids >> bit) & 1) << (bit // 3)
    packed = coords[0] + 256 * coords[1] + 65536 * coords[2]
    return np.pad(packed, (PER, PER)).astype(np.int32)


def tangent_tables():
    mean = 0.75 * (np.arange(512) + 0.5)
    s = np.sqrt(mean)
    beta = 0.5 * np.exp(-s) / (LOG2E * LOG2E) / FACTOR
    alpha = -(1 + s) * np.exp(-s) / FACTOR - beta * mean * LOG2E * LOG2E
    alpha = np.append(alpha, -LOG2E)
    return alpha.astype(np.float32), beta.astype(np.float32)


def rounded(x):
    return x.astype(BF).astype(F32)


def split2(x):
    high = rounded(x)
    return jnp.concatenate([high, x - high], axis=0).astype(BF)


def split3(x):
    first = rounded(x)
    rest = x - first
    second = rounded(rest)
    return first, second, rounded(rest - second)


def source_pieces(w):
    a, b, c = split3(w)
    return jnp.concatenate([a, b, a, b, c, a], axis=0)


def target_pieces(u):
    a, b, c = split3(u)
    return jnp.concatenate([a, a, b, b, a, c], axis=0)


def rows_of(shape):
    return lax.broadcasted_iota(jnp.int32, shape, 0)


def source_rows(x):
    row = rows_of(x.shape)
    x = jnp.where(row < 3, x, 0.0)
    norm = KAPPA * jnp.sum(x * x, axis=0, keepdims=True)
    return jnp.where(row == 3, norm, jnp.where(row == 4, 1.0, x))


def target_rows(x):
    row = rows_of(x.shape)
    x = jnp.where(row < 3, x, 0.0)
    norm = KAPPA * jnp.sum(x * x, axis=0, keepdims=True)
    return jnp.where(row == 4, norm, jnp.where(row == 3, 1.0, (-2.0 * KAPPA) * x))


def kernel_value(q, shift):
    y = shift - q * lax.rsqrt(q)
    return y * jnp.exp2(y)


def halves(x):
    high = x.astype(BF)
    return high, (x - high.astype(F32)).astype(BF)


def dot(a, b):
    return jnp.dot(a, b, preferred_element_type=F32)


def dot_nt(a, b):
    return lax.dot_general(a, b, NT, preferred_element_type=F32)


def fold(x):
    return x[:RHS] + x[RHS:]


def body(
    points,
    rhs_hbm,
    start,
    leaf_skel,
    mid_skel,
    top_skel,
    basis_hbm,
    transfer_hbm,
    mid_transfer,
    noise,
    near,
    near_count,
    far_leaf,
    far_count,
    far_mid,
    far_top,
    corners,
    alphas,
    betas,
    first,
    image,
    step,
    remainder0,
    remainder1,
    far_high,
    far_low,
    mid_high,
    mid_low,
    top_high,
    top_low,
    halo1,
    halo2,
    gather1,
    gather2,
    mids2,
    all1,
    all2,
    sums1,
    sums2,
    field,
    wfeat,
    ufeat,
    urows,
    moments,
    skel_rows,
    tangent_a,
    tangent_b,
    skel_feat,
    mid_feat,
    top_feat,
    top_tiles,
    basis_high,
    basis_low,
    transfer2,
    near_acc,
    local,
    rhs,
    basis,
    transfer,
    fetch_sem,
    halo_send,
    halo_recv,
    coef_send,
    coef_recv,
    all_send,
    all_recv,
    sum_send,
    sum_recv,
    tot_send,
    tot_recv,
):
    g = lax.axis_index("grp")
    i = lax.axis_index("leaf")
    lane = lax.broadcasted_iota(jnp.int32, (RHS, 128), 1)
    low_lanes = lane < RANK
    tile_shape = (RHS, 128)

    def peer_leaf(k):
        return (g, lax.rem(i + k, GSIZE))

    def peer_grp(k):
        return (lax.rem(g + k, GROUPS), i)

    up = i + 1
    down = i + GSIZE - 1
    after = (lax.rem(g + lax.div(up, GSIZE), GROUPS), lax.rem(up, GSIZE))
    before = (lax.rem(g + GROUPS - 1 + lax.div(down, GSIZE), GROUPS), lax.rem(down, GSIZE))

    fetches = [
        pltpu.make_async_copy(src, dst, fetch_sem.at[n])
        for n, (src, dst) in enumerate(
            ((basis_hbm, basis), (transfer_hbm, transfer), (rhs_hbm, rhs))
        )
    ]
    for copy in fetches:
        copy.start()
    barrier = pltpu.get_barrier_semaphore()
    partners = (
        [peer_leaf(k) for k in range(1, GSIZE)]
        + [peer_grp(k) for k in range(1, GROUPS)]
        + [after, before]
    )
    for partner in partners:
        pl.semaphore_signal(barrier, inc=1, device_id=partner, device_id_type=MESH)

    def remote(src, dst, send, recv, device):
        return pltpu.make_async_remote_copy(
            src_ref=src,
            dst_ref=dst,
            send_sem=send,
            recv_sem=recv,
            device_id=device,
            device_id_type=MESH,
        )

    def halo_copies(window, phase, *where):
        own, low, high = (window.at[(block,) + where] for block in (1, 0, 2))
        return [
            remote(own, low, halo_send.at[phase, 0], halo_recv.at[phase, 0], after),
            remote(own, high, halo_send.at[phase, 1], halo_recv.at[phase, 1], before),
        ]

    def leaf_copies(buffer, send, recv, phase):
        own = buffer.at[i]
        return [
            remote(own, own, send.at[phase, k], recv.at[phase, i], peer_leaf(k))
            for k in range(1, GSIZE)
        ]

    def wait_leaf(buffer, send, recv, phase):
        for k in range(1, GSIZE):
            src = lax.rem(i + k, GSIZE)
            theirs = buffer.at[src]
            remote(theirs, theirs, send.at[phase, k], recv.at[phase, src], peer_leaf(k)).wait_recv()

    def grp_copies(buffer, send, recv, phase):
        return [
            remote(buffer.at[g], buffer.at[g], send.at[phase, k], recv.at[phase, g], peer_grp(k))
            for k in range(1, GROUPS)
        ]

    def wait_grp(buffer, send, recv, phase):
        for k in range(1, GROUPS):
            src = lax.rem(g + k, GROUPS)
            remote(
                buffer.at[src], buffer.at[src], send.at[phase, k], recv.at[phase, src], peer_grp(k)
            ).wait_recv()

    pending = []

    def launch(copies):
        for copy in copies:
            copy.start()
        pending.extend(copies)

    def coefficients(read, tiles, first_tile, mid_tile):
        total = jnp.zeros((2 * RHS, RANK), F32)
        for p in range(PER // 2):
            parts = []
            for side in range(2):
                leaf = 2 * p + side
                v = split2(read(leaf))
                field[PER + leaf] = v
                parts.append(fold(dot_nt(v, basis_high[leaf]) + dot_nt(v, basis_low[leaf])))
            tile = jnp.concatenate(parts, axis=1)
            tiles[first_tile + p] = tile
            c = split2(tile)
            for part in range(2):
                total += dot_nt(c, transfer2[part, :, 128 * p : 128 * (p + 1)])
        mid = fold(total)
        m = split2(mid)
        high, low = halves(mid_transfer[0])
        top = fold(dot_nt(m, high) + dot_nt(m, low))
        mid_tile[...] = jnp.concatenate([mid, top], axis=1)

    def column(leaf):
        return pl.ds(pl.multiple_of(leaf * LEAF, LEAF), LEAF)

    width, span = PER * LEAF, PACKED // 3
    halo1[1, :, 0:width] = start[...]
    for c in range(3):
        for r in range(8):
            halo1[1, r : r + 1, width + c * span : width + (c + 1) * span] = points[
                c : c + 1, r * span : (r + 1) * span
            ]
    for copy in fetches:
        copy.wait()
    for leaf in range(PER):
        high, low = halves(basis[leaf])
        basis_high[leaf] = high
        basis_low[leaf] = low
    for p in range(PER // 2):
        both = jnp.concatenate([transfer[2 * p], transfer[2 * p + 1]], axis=1)
        high, low = halves(both)
        transfer2[0, :, 128 * p : 128 * (p + 1)] = high
        transfer2[1, :, 128 * p : 128 * (p + 1)] = low
    pl.semaphore_wait(barrier, len(partners))
    launch(halo_copies(halo1, 0))

    own_gather = gather1.at[i]
    own_skel = []
    for p in range(PER // 2):
        tile = jnp.concatenate(
            [leaf_skel[:, 128 * p : 128 * (p + 1)], jnp.zeros((5, 128), F32)], axis=0
        )
        own_skel.append(tile)
        own_gather[2 + PER // 2 : 5 + PER // 2, p : p + 1, :] = tile[0:3].reshape(3, 1, 128)
    own_gather[1] = jnp.zeros((8, 128), F32)
    own_gather[1, 0:3, 0:RANK] = mid_skel[...]
    coefficients(lambda leaf: start[:, LEAF * leaf : LEAF * (leaf + 1)], own_gather, 2, own_gather.at[0])
    centre = jnp.concatenate([jnp.floor(points[:, 0:1]), jnp.zeros((5, 1), F32)], axis=0)
    device = g * GSIZE + i
    base = device * PER

    def leaf_points(block, l):
        per_row = span // LEAF
        row, place = lax.div(l, per_row), lax.rem(l, per_row) * LEAF
        out = jnp.zeros((8, LEAF), F32)
        for c in range(3):
            cols = pl.ds(pl.multiple_of(width + c * span + place, LEAF), LEAF)
            out = jnp.where(rows_of((8, LEAF)) == c, halo1[block, pl.ds(row, 1), cols], out)
        return out

    def window_features(leaf, block, place):
        x = leaf_points(block, place) - centre
        wfeat[leaf] = source_pieces(source_rows(x)).T.astype(BF)
        return x

    def tangents(l):
        a = corners[base + PER + l] + 0x202020
        count = near_count[l]
        for s in range(NEAR):
            d = a - corners[base + near[l, s]]
            dx = (d & 255) - 32
            dy = ((d >> 8) & 255) - 32
            dz = (d >> 16) - 32
            d2 = jnp.minimum(dx * dx + dy * dy + dz * dz, 511)
            live = s < count
            tangent_a[l, s] = jnp.where(live, alphas[d2], 0.0)
            tangent_b[l, s] = jnp.where(live, betas[d2], 0.0)

    def own_features(n, carry):
        for t in range(4):
            l = 4 * n + t
            x = window_features(PER + l, 1, l)
            u = target_rows(x)
            urows[l] = u
            ufeat[l] = target_pieces(u).astype(BF)
            tangents(l)
        return carry

    lax.fori_loop(0, PER // 4, own_features, 0)
    for p in range(PER // 2):
        u = target_pieces(target_rows(own_skel[p] - centre))
        skel_feat[128 * p : 128 * (p + 1), :] = u.T.astype(BF)
    u = target_pieces(target_rows(own_gather[1] - centre))
    mid_feat[...] = u.T.astype(BF)
    for p in range(GROUPS // 2):
        top_tiles[p] = jnp.concatenate(
            [top_skel[:, 128 * p : 128 * (p + 1)], jnp.zeros((5, 128), F32)], axis=0
        )
    tile = top_tiles[lax.div(g, 2)]
    tile = jnp.where(lax.rem(g, 2) == 0, tile, pltpu.roll(tile, RANK, 1))
    top_feat[...] = target_pieces(target_rows(tile - centre)).T.astype(BF)

    def field_moments(first_leaf):
        lane8 = lax.broadcasted_iota(jnp.int32, (RHS, 8), 1)

        def some(n, carry):
            for t in range(8):
                leaf = first_leaf + 8 * n + t
                r = fold(dot(field[leaf], wfeat[leaf]))
                m = r[:, 0:8] + r[:, 8:16] + r[:, 32:40]
                moments[leaf, 0] = m
                moments[leaf, 1] = jnp.where(lane8 == 3, m[:, 4:5], 0.0)
            return carry

        lax.fori_loop(0, PER // 8, some, 0)

    field_moments(PER)
    for copy in halo_copies(halo1, 0):
        copy.wait_recv()
    launch(leaf_copies(gather1, coef_send, coef_recv, 0))

    def edge_features(n, carry):
        for t in range(4):
            l = 4 * n + t
            for block in (0, 2):
                leaf = block * PER + l
                window_features(leaf, block, l)
                field[leaf] = split2(halo1[block, :, column(l)])
        return carry

    lax.fori_loop(0, PER // 4, edge_features, 0)
    field_moments(0)
    field_moments(2 * PER)

    shift = alphas[512]
    remainders = (remainder0, remainder1)

    def evaluate(n, side):
        l = 2 * n + side
        feat = ufeat[l]
        for c in range(0, LEAF, 64):
            for t in range(NEAR):
                q = jnp.maximum(dot(wfeat[near[l, t], c : c + 64, :], feat), TINY)
                r = kernel_value(q, shift) - (q * tangent_b[l, t] + tangent_a[l, t])
                row = (n * NEAR + t) * LEAF + c
                remainders[side][pl.ds(pl.multiple_of(row, 64), 64), :] = r.astype(BF)

    def multiply(n, side):
        l = 2 * n + side
        cols = []
        live = near_count[l]
        for t in range(NEAR):
            v = field[near[l, t]]
            cols.append(jnp.where(t < live, v, jnp.zeros_like(v)))
        rows = pl.ds(pl.multiple_of(n * NEAR * LEAF, LEAF), NEAR * LEAF)
        near_acc[l] = dot(jnp.concatenate(cols, axis=1), remainders[side][rows, :])

    def tangent_part(l):
        total = jnp.zeros((RHS, 8), F32)
        for s in range(NEAR):
            j = near[l, s]
            total += tangent_b[l, s] * moments[j, 0] + tangent_a[l, s] * moments[j, 1]
        out = total[:, 0:1] * urows[l, 0:1, :]
        for k in range(1, 5):
            out += total[:, k : k + 1] * urows[l, k : k + 1, :]
        return out

    remainder1[(PER // 2 - 1) * NEAR * LEAF :, :] = jnp.zeros((NEAR * LEAF, LEAF), BF)

    def near_step(n, carry):
        multiply(lax.rem(n + PER // 2 - 1, PER // 2), 1)
        evaluate(n, 0)
        multiply(n, 0)
        evaluate(n, 1)
        return carry

    lax.fori_loop(0, PER // 4, near_step, 0)
    wait_leaf(gather1, coef_send, coef_recv, 0)
    for m in range(GSIZE):
        all1[g, m] = gather1[m, 0:2]
    launch(grp_copies(all1, all_send, all_recv, 0))
    lax.fori_loop(PER // 4, PER // 2, near_step, 0)
    multiply(PER // 2 - 1, 1)

    def moved(tile, index, want):
        return jnp.where((index & 1) == want, tile, pltpu.roll(tile, RANK, 1))

    def joined(first_tile, second_tile):
        return jnp.where(low_lanes, first_tile, second_tile)

    def far_tiles(feat, rows):
        q = jnp.maximum(dot(feat, source_pieces(rows).astype(BF)), TINY)
        return halves(kernel_value(q, shift))

    def skeleton_rows(n, carry):
        for t in range(PER // 2):
            parts = [gather1[n, 2 + PER // 2 + c, t : t + 1, :] for c in range(3)]
            tile = jnp.concatenate(parts + [jnp.zeros((5, 128), F32)], axis=0)
            skel_rows[n * (PER // 2) + t] = source_rows(tile - centre)
        return carry

    def far_matrix(lp, carry):
        for side in range(4):
            l = 4 * lp + side
            feat = skel_feat[pl.ds(pl.multiple_of(l * RANK, RANK), RANK), :]
            for p in range(FARL // 2):
                j1, j2 = far_leaf[l, 2 * p], far_leaf[l, 2 * p + 1]
                rows = joined(
                    moved(skel_rows[j1 >> 1], j1, 0), moved(skel_rows[j2 >> 1], j2, 1)
                )
                high, low = far_tiles(feat, rows)
                far_high[l, :, 128 * p : 128 * (p + 1)] = high
                far_low[l, :, 128 * p : 128 * (p + 1)] = low
        far_leaves(lp, lambda j: gather1[j >> 4, 2 + ((j >> 1) & 7)])
        return carry

    def far_leaves(n, read):
        for q in range(2):
            lp = 2 * n + q
            parts = []
            for side in range(2):
                l = 2 * lp + side
                count = far_count[l]
                cols = []
                for p in range(FARL // 2):
                    s = 2 * p
                    j1, j2 = far_leaf[l, s], far_leaf[l, s + 1]
                    tile = joined(moved(read(j1), j1, 0), moved(read(j2), j2, 1))
                    slot = s + jnp.where(low_lanes, 0, 1)
                    cols.append(split2(jnp.where(slot < count, tile, 0.0)))
                c = jnp.concatenate(cols, axis=1)
                parts.append(dot_nt(far_high[l], c) + dot_nt(far_low[l], c))
            local[lp] = -FACTOR * fold(jnp.concatenate(parts, axis=0).T)

    def upper_matrix(buffer):
        def read_mid(m):
            return source_rows(buffer[m >> 4, m & 15, 1] - centre)

        for p in range(FARM // 2):
            one, two = read_mid(far_mid[0, 2 * p]), read_mid(far_mid[0, 2 * p + 1])
            high, low = far_tiles(mid_feat[0:RANK, :], joined(one, pltpu.roll(two, RANK, 1)))
            mid_high[:, 128 * p : 128 * (p + 1)] = high
            mid_low[:, 128 * p : 128 * (p + 1)] = low

        def read_top(j, want):
            return moved(source_rows(top_tiles[j >> 1] - centre), j, want)

        for p in range(2):
            j1 = far_top[0, 2 * p]
            j2 = far_top[0, min(2 * p + 1, FART - 1)]
            high, low = far_tiles(top_feat[0:RANK, :], joined(read_top(j1, 0), read_top(j2, 1)))
            top_high[:, 128 * p : 128 * (p + 1)] = high
            top_low[:, 128 * p : 128 * (p + 1)] = low

    def upper_local(read, read_top):
        cols = []
        for p in range(FARM // 2):
            m1, m2 = far_mid[0, 2 * p], far_mid[0, 2 * p + 1]
            cols.append(split2(joined(read(m1, 0), read(m2, 1))))
        c = jnp.concatenate(cols, axis=1)
        mid_far = -FACTOR * fold(dot_nt(c, mid_high[...]) + dot_nt(c, mid_low[...]))

        t0, t1, t2 = (read_top(far_top[0, s]) for s in range(FART))
        cols = [
            split2(joined(pltpu.roll(t0, RANK, 1), t1)),
            split2(joined(pltpu.roll(t2, RANK, 1), jnp.zeros((RHS, 128), F32))),
        ]
        c = jnp.concatenate(cols, axis=1)
        top_far = -FACTOR * fold(dot_nt(c, top_high[...]) + dot_nt(c, top_low[...]))
        high, low = halves(mid_transfer[0])
        t = split2(top_far)
        return mid_far + fold(dot(t, high) + dot(t, low))

    def down(read_mid, read_top):
        m = split2(upper_local(read_mid, read_top))
        for p in range(PER // 2):
            down_part = sum(dot(m, transfer2[part, :, 128 * p : 128 * (p + 1)]) for part in range(2))
            local[p] += fold(down_part)

    def finish(n, store):
        for t in range(4):
            l = 4 * n + t
            tile = local[2 * n + t // 2]
            c = split2(tile[:, RANK * (t % 2) : RANK * (t % 2 + 1)])
            far = fold(dot(c, basis_high[l]) + dot(c, basis_low[l]))
            near_part = -FACTOR * (fold(near_acc[l]) + tangent_part(l))
            store(l, near_part + far)

    lax.fori_loop(0, GSIZE, skeleton_rows, 0)
    lax.fori_loop(0, PER // 4, far_matrix, 0)
    wait_grp(all1, all_send, all_recv, 0)
    upper_matrix(all1)
    noise_value = noise[0]

    def first_leaves(n, carry):
        def store(l, value):
            cols = column(l)
            r = rhs[:, cols] - (noise_value * start[:, cols] + value)
            first[:, cols] = r
            halo2[1, :, cols] = r

        finish(n, store)
        return carry

    left, right = (slice(None), slice(0, width // 2)), (slice(None), slice(width // 2, width))
    def mid1(m, want):
        tile = all1[m >> 4, m & 15, 0]
        return pltpu.roll(tile, RANK, 1) if want else tile

    def top1(j):
        total = all1[j, 0, 0]
        for m in range(1, GSIZE):
            total += all1[j, m, 0]
        return total

    down(mid1, top1)
    lax.fori_loop(0, PER // 8, first_leaves, 0)
    launch(halo_copies(halo2, 1, *left))
    lax.fori_loop(PER // 8, PER // 4, first_leaves, 0)
    launch(halo_copies(halo2, 2, *right))

    coefficients(lambda leaf: first[:, LEAF * leaf : LEAF * (leaf + 1)], gather2.at[i], 0, mids2.at[i])
    launch(leaf_copies(mids2, sum_send, sum_recv, 1))
    launch(leaf_copies(gather2, coef_send, coef_recv, 1))
    field_moments(PER)
    for copy in halo_copies(halo2, 1, *left) + halo_copies(halo2, 2, *right):
        copy.wait_recv()

    def edge_fields(n, carry):
        for t in range(4):
            l = 4 * n + t
            for block in (0, 2):
                field[block * PER + l] = split2(halo2[block, :, column(l)])
        return carry

    lax.fori_loop(0, PER // 4, edge_fields, 0)
    field_moments(0)
    field_moments(2 * PER)

    def near_again(n, carry):
        multiply(n, 0)
        multiply(n, 1)
        return carry

    lax.fori_loop(0, PER // 4, near_again, 0)
    wait_leaf(mids2, sum_send, sum_recv, 1)
    group_top = jnp.zeros(tile_shape, F32)
    for p in range(GSIZE // 2):
        one, two = mids2[2 * p], mids2[2 * p + 1]
        all2[g, p] = joined(one, pltpu.roll(two, RANK, 1))
        group_top += one + two
    all2[g, GSIZE // 2] = group_top
    launch(grp_copies(all2, all_send, all_recv, 1))
    wait_leaf(gather2, coef_send, coef_recv, 1)

    def near_and_far(n, carry):
        multiply(PER // 4 + n, 0)
        multiply(PER // 4 + n, 1)
        far_leaves(n, lambda j: gather2[j >> 4, (j >> 1) & 7])
        return carry

    lax.fori_loop(0, PER // 4, near_and_far, 0)
    wait_grp(all2, all_send, all_recv, 1)

    def image_leaves(n, carry):
        def store(l, value):
            cols = column(l)
            image[:, cols] = noise_value * first[:, cols] + value

        finish(n, store)
        return carry

    down(
        lambda m, want: moved(all2[m >> 4, (m & 15) >> 1], m, want),
        lambda j: all2[j, GSIZE // 2],
    )
    lax.fori_loop(0, PER // 4, image_leaves, 0)

    dots = jnp.zeros((RHS, LEAF), F32)
    squares = jnp.zeros((RHS, LEAF), F32)
    for l in range(PER):
        cols = slice(LEAF * l, LEAF * (l + 1))
        y = image[:, cols]
        dots += first[:, cols] * y
        squares += y * y
    sums1[i] = jnp.where(
        low_lanes,
        jnp.sum(dots, axis=1, keepdims=True),
        jnp.sum(squares, axis=1, keepdims=True),
    )
    launch(leaf_copies(sums1, sum_send, sum_recv, 0))
    wait_leaf(sums1, sum_send, sum_recv, 0)
    total = sums1[0]
    for k in range(1, GSIZE):
        total += sums1[k]
    sums2[g] = total
    launch(grp_copies(sums2, tot_send, tot_recv, 0))
    wait_grp(sums2, tot_send, tot_recv, 0)
    total = sums2[0]
    for k in range(1, GROUPS):
        total += sums2[k]
    total = total / (LEAVES * LEAF)
    alpha = total[:, 0:1] / (total[:, RANK : RANK + 1] + 1e-6)
    step[...] = jnp.broadcast_to(alpha, (RHS, 128))
    for copy in pending:
        copy.wait_send()


def shards(*args):
    smem = pl.BlockSpec(memory_space=pltpu.SMEM)
    vmem = pl.BlockSpec(memory_space=pltpu.VMEM)
    hbm = pl.BlockSpec(memory_space=pl.ANY)
    alphas, betas = tangent_tables()
    tables = (jnp.asarray(morton_table()), jnp.asarray(alphas), jnp.asarray(betas))
    out = jax.ShapeDtypeStruct((RHS, PER * LEAF), F32)
    tile = (8, 128)

    def buffer(shape, dtype=F32):
        return pltpu.VMEM(shape, dtype)

    def sems(*shape):
        return pltpu.SemaphoreType.DMA(shape)

    scratch = [
        buffer((PER // 2 * NEAR * LEAF, LEAF), BF),
        buffer((PER // 2 * NEAR * LEAF, LEAF), BF),
        buffer((PER, RANK, FARL * RANK), BF),
        buffer((PER, RANK, FARL * RANK), BF),
        buffer((RANK, FARM * RANK), BF),
        buffer((RANK, FARM * RANK), BF),
        buffer((RANK, 4 * RANK), BF),
        buffer((RANK, 4 * RANK), BF),
        buffer((3, 8, PER * LEAF + PACKED)),
        buffer((3, 8, PER * LEAF)),
        buffer((GSIZE, TILES1) + tile),
        buffer((GSIZE, TILES2) + tile),
        buffer((GSIZE,) + tile),
        buffer((GROUPS, GSIZE, 2) + tile),
        buffer((GROUPS, GSIZE // 2 + 1) + tile),
        buffer((GSIZE,) + tile),
        buffer((GROUPS,) + tile),
        buffer((WIN, 2 * RHS, LEAF), BF),
        buffer((WIN, LEAF, PIECES), BF),
        buffer((PER, PIECES, LEAF), BF),
        buffer((PER, 8, LEAF)),
        buffer((WIN, 2, RHS, 8)),
        buffer((GSIZE * PER // 2,) + tile),
        pltpu.SMEM((PER, NEAR), F32),
        pltpu.SMEM((PER, NEAR), F32),
        buffer((PER * RANK, PIECES), BF),
        buffer((128, PIECES), BF),
        buffer((128, PIECES), BF),
        buffer((GROUPS // 2,) + tile),
        buffer((PER, RANK, LEAF), BF),
        buffer((PER, RANK, LEAF), BF),
        buffer((2, RANK, PER * RANK), BF),
        buffer((PER, 2 * RHS, LEAF)),
        buffer((PER // 2,) + tile),
        buffer((RHS, PER * LEAF)),
        buffer((PER, RANK, LEAF)),
        buffer((PER, RANK, RANK)),
        sems(3),
        sems(3, 2),
        sems(3, 2),
        sems(2, GSIZE),
        sems(2, GSIZE),
        sems(2, GROUPS),
        sems(2, GROUPS),
        sems(2, GSIZE),
        sems(2, GSIZE),
        sems(1, GROUPS),
        sems(1, GROUPS),
    ]
    first, image, step = pl.pallas_call(
        body,
        out_shape=(out, out, jax.ShapeDtypeStruct(tile, F32)),
        in_specs=[hbm if n in (1, 6, 7) else vmem for n in range(9)] + [smem] * 10,
        out_specs=(vmem, vmem, vmem),
        scratch_shapes=scratch,
        compiler_params=pltpu.CompilerParams(
            collective_id=0, has_side_effects=True, vmem_limit_bytes=61 << 20
        ),
    )(*args, *tables)
    alpha = step[:, 0:1]
    return args[2] + alpha * first, first - alpha * image


def solution(mesh):
    columns = P(None, ("grp", "leaf"))
    blocks = P(("grp", "leaf"), None, None)
    lists = P(("grp", "leaf"), None)
    return jax.shard_map(
        shards,
        mesh=mesh,
        in_specs=(
            columns,
            columns,
            columns,
            columns,
            columns,
            P(),
            blocks,
            blocks,
            blocks,
            P(),
            lists,
            P(("grp", "leaf")),
            lists,
            P(("grp", "leaf")),
            lists,
            P("grp", None),
        ),
        out_specs=(columns, columns),
        check_vma=False,
    )
```

```python
import functools
import math

import jax
import jax.numpy as jnp
import numpy as np
from jax import lax
from jax.experimental import pallas as pl
from jax.experimental.pallas import tpu as pltpu
from jax.sharding import PartitionSpec as P

BF = jnp.bfloat16
F32 = jnp.float32
MESH = pl.DeviceIdType.MESH
NT = (((1,), (1,)), ((), ()))

LEAF = 256
RANK = 64
RHS = 8
PER = 16
NEAR = 16
FARL = 32
FARM = 16
FART = 3
GROUPS = 8
GSIZE = 16
LEAVES = 2048
WIN = 3 * PER
PIECES = 48
TILES1 = 5 + PER // 2
TILES2 = PER // 2
PACKED = 3 * PER * LEAF // 8

LOG2E = math.log2(math.e)
KAPPA = 0.75 * LOG2E * LOG2E
FACTOR = math.e * math.log(2.0)
TINY = 1e-30


def morton_table():
    ids = np.arange(LEAVES)
    coords = [np.zeros_like(ids) for _ in range(3)]
    for bit in range(30):
        coords[bit % 3] += ((ids >> bit) & 1) << (bit // 3)
    packed = coords[0] + 256 * coords[1] + 65536 * coords[2]
    return np.pad(packed, (PER, PER)).astype(np.int32)


def tangent_tables():
    mean = 0.75 * (np.arange(512) + 0.5)
    s = np.sqrt(mean)
    beta = 0.5 * np.exp(-s) / (LOG2E * LOG2E) / FACTOR
    alpha = -(1 + s) * np.exp(-s) / FACTOR - beta * mean * LOG2E * LOG2E
    alpha = np.append(alpha, -LOG2E)
    return alpha.astype(np.float32), beta.astype(np.float32)


def rounded(x):
    return x.astype(BF).astype(F32)


def split2(x):
    high = rounded(x)
    return jnp.concatenate([high, x - high], axis=0).astype(BF)


def split3(x):
    first = rounded(x)
    rest = x - first
    second = rounded(rest)
    return first, second, rounded(rest - second)


def source_pieces(w):
    a, b, c = split3(w)
    return jnp.concatenate([a, b, a, b, c, a], axis=0)


def target_pieces(u):
    a, b, c = split3(u)
    return jnp.concatenate([a, a, b, b, a, c], axis=0)


def rows_of(shape):
    return lax.broadcasted_iota(jnp.int32, shape, 0)


def source_rows(x):
    row = rows_of(x.shape)
    x = jnp.where(row < 3, x, 0.0)
    norm = KAPPA * jnp.sum(x * x, axis=0, keepdims=True)
    return jnp.where(row == 3, norm, jnp.where(row == 4, 1.0, x))


def target_rows(x):
    row = rows_of(x.shape)
    x = jnp.where(row < 3, x, 0.0)
    norm = KAPPA * jnp.sum(x * x, axis=0, keepdims=True)
    return jnp.where(row == 4, norm, jnp.where(row == 3, 1.0, (-2.0 * KAPPA) * x))


def kernel_value(q, shift):
    y = shift - q * lax.rsqrt(q)
    return y * jnp.exp2(y)


def halves(x):
    high = x.astype(BF)
    return high, (x - high.astype(F32)).astype(BF)


def dot(a, b):
    return jnp.dot(a, b, preferred_element_type=F32)


def dot_nt(a, b):
    return lax.dot_general(a, b, NT, preferred_element_type=F32)


def fold(x):
    return x[:RHS] + x[RHS:]


def body(
    points,
    rhs_hbm,
    start,
    leaf_skel,
    mid_skel,
    top_skel,
    basis_hbm,
    transfer_hbm,
    mid_transfer,
    noise,
    near,
    near_count,
    far_leaf,
    far_count,
    far_mid,
    far_top,
    corners,
    alphas,
    betas,
    first,
    image,
    step,
    remainder0,
    remainder1,
    far_high,
    far_low,
    mid_high,
    mid_low,
    top_high,
    top_low,
    halo1,
    halo2,
    gather1,
    gather2,
    mids2,
    all1,
    all2,
    sums1,
    sums2,
    field,
    wfeat,
    ufeat,
    urows,
    moments,
    skel_rows,
    tangent_a,
    tangent_b,
    skel_feat,
    mid_feat,
    top_feat,
    top_tiles,
    basis_high,
    basis_low,
    transfer2,
    near_acc,
    local,
    rhs,
    basis,
    transfer,
    fetch_sem,
    halo_send,
    halo_recv,
    coef_send,
    coef_recv,
    all_send,
    all_recv,
    sum_send,
    sum_recv,
    tot_send,
    tot_recv,
):
    g = lax.axis_index("grp")
    i = lax.axis_index("leaf")
    lane = lax.broadcasted_iota(jnp.int32, (RHS, 128), 1)
    low_lanes = lane < RANK
    tile_shape = (RHS, 128)

    def peer_leaf(k):
        return (g, lax.rem(i + k, GSIZE))

    def peer_grp(k):
        return (lax.rem(g + k, GROUPS), i)

    up = i + 1
    down = i + GSIZE - 1
    after = (lax.rem(g + lax.div(up, GSIZE), GROUPS), lax.rem(up, GSIZE))
    before = (lax.rem(g + GROUPS - 1 + lax.div(down, GSIZE), GROUPS), lax.rem(down, GSIZE))

    fetches = [
        pltpu.make_async_copy(src, dst, fetch_sem.at[n])
        for n, (src, dst) in enumerate(
            ((basis_hbm, basis), (transfer_hbm, transfer), (rhs_hbm, rhs))
        )
    ]
    for copy in fetches:
        copy.start()
    barrier = pltpu.get_barrier_semaphore()
    partners = (
        [peer_leaf(k) for k in range(1, GSIZE)]
        + [peer_grp(k) for k in range(1, GROUPS)]
        + [after, before]
    )
    for partner in partners:
        pl.semaphore_signal(barrier, inc=1, device_id=partner, device_id_type=MESH)

    def remote(src, dst, send, recv, device):
        return pltpu.make_async_remote_copy(
            src_ref=src,
            dst_ref=dst,
            send_sem=send,
            recv_sem=recv,
            device_id=device,
            device_id_type=MESH,
        )

    def halo_copies(window, phase, *where):
        own, low, high = (window.at[(block,) + where] for block in (1, 0, 2))
        return [
            remote(own, low, halo_send.at[phase, 0], halo_recv.at[phase, 0], after),
            remote(own, high, halo_send.at[phase, 1], halo_recv.at[phase, 1], before),
        ]

    def leaf_copies(buffer, send, recv, phase):
        own = buffer.at[i]
        return [
            remote(own, own, send.at[phase, k], recv.at[phase, i], peer_leaf(k))
            for k in range(1, GSIZE)
        ]

    def wait_leaf(buffer, send, recv, phase):
        for k in range(1, GSIZE):
            src = lax.rem(i + k, GSIZE)
            theirs = buffer.at[src]
            remote(theirs, theirs, send.at[phase, k], recv.at[phase, src], peer_leaf(k)).wait_recv()

    def grp_copies(buffer, send, recv, phase):
        return [
            remote(buffer.at[g], buffer.at[g], send.at[phase, k], recv.at[phase, g], peer_grp(k))
            for k in range(1, GROUPS)
        ]

    def wait_grp(buffer, send, recv, phase):
        for k in range(1, GROUPS):
            src = lax.rem(g + k, GROUPS)
            remote(
                buffer.at[src], buffer.at[src], send.at[phase, k], recv.at[phase, src], peer_grp(k)
            ).wait_recv()

    pending = []

    def launch(copies):
        for copy in copies:
            copy.start()
        pending.extend(copies)

    def coefficients(read, tiles, first_tile, mid_tile):
        total = jnp.zeros((2 * RHS, RANK), F32)
        for p in range(PER // 2):
            parts = []
            for side in range(2):
                leaf = 2 * p + side
                v = split2(read(leaf))
                field[PER + leaf] = v
                parts.append(fold(dot_nt(v, basis_high[leaf]) + dot_nt(v, basis_low[leaf])))
            tile = jnp.concatenate(parts, axis=1)
            tiles[first_tile + p] = tile
            c = split2(tile)
            for part in range(2):
                total += dot_nt(c, transfer2[part, :, 128 * p : 128 * (p + 1)])
        mid = fold(total)
        m = split2(mid)
        high, low = halves(mid_transfer[0])
        top = fold(dot_nt(m, high) + dot_nt(m, low))
        mid_tile[...] = jnp.concatenate([mid, top], axis=1)

    def column(leaf):
        return pl.ds(pl.multiple_of(leaf * LEAF, LEAF), LEAF)

    width, span = PER * LEAF, PACKED // 3
    halo1[1, :, 0:width] = start[...]
    for c in range(3):
        for r in range(8):
            halo1[1, r : r + 1, width + c * span : width + (c + 1) * span] = points[
                c : c + 1, r * span : (r + 1) * span
            ]
    for copy in fetches:
        copy.wait()
    for leaf in range(PER):
        high, low = halves(basis[leaf])
        basis_high[leaf] = high
        basis_low[leaf] = low
    for p in range(PER // 2):
        both = jnp.concatenate([transfer[2 * p], transfer[2 * p + 1]], axis=1)
        high, low = halves(both)
        transfer2[0, :, 128 * p : 128 * (p + 1)] = high
        transfer2[1, :, 128 * p : 128 * (p + 1)] = low
    pl.semaphore_wait(barrier, len(partners))
    launch(halo_copies(halo1, 0))

    own_gather = gather1.at[i]
    own_skel = []
    for p in range(PER // 2):
        tile = jnp.concatenate(
            [leaf_skel[:, 128 * p : 128 * (p + 1)], jnp.zeros((5, 128), F32)], axis=0
        )
        own_skel.append(tile)
        own_gather[2 + PER // 2 : 5 + PER // 2, p : p + 1, :] = tile[0:3].reshape(3, 1, 128)
    own_gather[1] = jnp.zeros((8, 128), F32)
    own_gather[1, 0:3, 0:RANK] = mid_skel[...]
    coefficients(lambda leaf: start[:, LEAF * leaf : LEAF * (leaf + 1)], own_gather, 2, own_gather.at[0])
    centre = jnp.concatenate([jnp.floor(points[:, 0:1]), jnp.zeros((5, 1), F32)], axis=0)
    device = g * GSIZE + i
    base = device * PER

    def leaf_points(block, l):
        per_row = span // LEAF
        row, place = lax.div(l, per_row), lax.rem(l, per_row) * LEAF
        out = jnp.zeros((8, LEAF), F32)
        for c in range(3):
            cols = pl.ds(pl.multiple_of(width + c * span + place, LEAF), LEAF)
            out = jnp.where(rows_of((8, LEAF)) == c, halo1[block, pl.ds(row, 1), cols], out)
        return out

    def window_features(leaf, block, place):
        x = leaf_points(block, place) - centre
        wfeat[leaf] = source_pieces(source_rows(x)).T.astype(BF)
        return x

    def tangents(l):
        a = corners[base + PER + l] + 0x202020
        count = near_count[l]
        for s in range(NEAR):
            d = a - corners[base + near[l, s]]
            dx = (d & 255) - 32
            dy = ((d >> 8) & 255) - 32
            dz = (d >> 16) - 32
            d2 = jnp.minimum(dx * dx + dy * dy + dz * dz, 511)
            live = s < count
            tangent_a[l, s] = jnp.where(live, alphas[d2], 0.0)
            tangent_b[l, s] = jnp.where(live, betas[d2], 0.0)

    def own_features(n, carry):
        for t in range(4):
            l = 4 * n + t
            x = window_features(PER + l, 1, l)
            u = target_rows(x)
            urows[l] = u
            ufeat[l] = target_pieces(u).astype(BF)
            tangents(l)
        return carry

    lax.fori_loop(0, PER // 4, own_features, 0)
    for p in range(PER // 2):
        u = target_pieces(target_rows(own_skel[p] - centre))
        skel_feat[128 * p : 128 * (p + 1), :] = u.T.astype(BF)
    u = target_pieces(target_rows(own_gather[1] - centre))
    mid_feat[...] = u.T.astype(BF)
    for p in range(GROUPS // 2):
        top_tiles[p] = jnp.concatenate(
            [top_skel[:, 128 * p : 128 * (p + 1)], jnp.zeros((5, 128), F32)], axis=0
        )
    tile = top_tiles[lax.div(g, 2)]
    tile = jnp.where(lax.rem(g, 2) == 0, tile, pltpu.roll(tile, RANK, 1))
    top_feat[...] = target_pieces(target_rows(tile - centre)).T.astype(BF)

    def field_moments(first_leaf):
        lane8 = lax.broadcasted_iota(jnp.int32, (RHS, 8), 1)

        def some(n, carry):
            for t in range(8):
                leaf = first_leaf + 8 * n + t
                r = fold(dot(field[leaf], wfeat[leaf]))
                m = r[:, 0:8] + r[:, 8:16] + r[:, 32:40]
                moments[leaf, 0] = m
                moments[leaf, 1] = jnp.where(lane8 == 3, m[:, 4:5], 0.0)
            return carry

        lax.fori_loop(0, PER // 8, some, 0)

    field_moments(PER)
    for copy in halo_copies(halo1, 0):
        copy.wait_recv()
    launch(leaf_copies(gather1, coef_send, coef_recv, 0))

    def edge_features(n, carry):
        for t in range(4):
            l = 4 * n + t
            for block in (0, 2):
                leaf = block * PER + l
                window_features(leaf, block, l)
                field[leaf] = split2(halo1[block, :, column(l)])
        return carry

    lax.fori_loop(0, PER // 4, edge_features, 0)
    field_moments(0)
    field_moments(2 * PER)

    shift = alphas[512]
    remainders = (remainder0, remainder1)

    def evaluate(n, side):
        l = 2 * n + side
        feat = ufeat[l]
        for c in range(0, LEAF, 64):
            for t in range(NEAR):
                q = jnp.maximum(dot(wfeat[near[l, t], c : c + 64, :], feat), TINY)
                r = kernel_value(q, shift) - (q * tangent_b[l, t] + tangent_a[l, t])
                row = (n * NEAR + t) * LEAF + c
                remainders[side][pl.ds(pl.multiple_of(row, 64), 64), :] = r.astype(BF)

    def multiply(n, side):
        l = 2 * n + side
        cols = []
        live = near_count[l]
        for t in range(NEAR):
            v = field[near[l, t]]
            cols.append(jnp.where(t < live, v, jnp.zeros_like(v)))
        rows = pl.ds(pl.multiple_of(n * NEAR * LEAF, LEAF), NEAR * LEAF)
        near_acc[l] = dot(jnp.concatenate(cols, axis=1), remainders[side][rows, :])

    def tangent_part(l):
        total = jnp.zeros((RHS, 8), F32)
        for s in range(NEAR):
            j = near[l, s]
            total += tangent_b[l, s] * moments[j, 0] + tangent_a[l, s] * moments[j, 1]
        out = total[:, 0:1] * urows[l, 0:1, :]
        for k in range(1, 5):
            out += total[:, k : k + 1] * urows[l, k : k + 1, :]
        return out

    remainder1[(PER // 2 - 1) * NEAR * LEAF :, :] = jnp.zeros((NEAR * LEAF, LEAF), BF)

    def near_step(n, carry):
        multiply(lax.rem(n + PER // 2 - 1, PER // 2), 1)
        evaluate(n, 0)
        multiply(n, 0)
        evaluate(n, 1)
        return carry

    lax.fori_loop(0, PER // 4, near_step, 0)
    wait_leaf(gather1, coef_send, coef_recv, 0)
    for m in range(GSIZE):
        all1[g, m] = gather1[m, 0:2]
    launch(grp_copies(all1, all_send, all_recv, 0))
    lax.fori_loop(PER // 4, PER // 2, near_step, 0)
    multiply(PER // 2 - 1, 1)

    def moved(tile, index, want):
        return jnp.where((index & 1) == want, tile, pltpu.roll(tile, RANK, 1))

    def joined(first_tile, second_tile):
        return jnp.where(low_lanes, first_tile, second_tile)

    def far_tiles(feat, rows):
        q = jnp.maximum(dot(feat, source_pieces(rows).astype(BF)), TINY)
        return halves(kernel_value(q, shift))

    def skeleton_rows(n, carry):
        for t in range(PER // 2):
            parts = [gather1[n, 2 + PER // 2 + c, t : t + 1, :] for c in range(3)]
            tile = jnp.concatenate(parts + [jnp.zeros((5, 128), F32)], axis=0)
            skel_rows[n * (PER // 2) + t] = source_rows(tile - centre)
        return carry

    def far_matrix(lp, carry):
        for side in range(4):
            l = 4 * lp + side
            feat = skel_feat[pl.ds(pl.multiple_of(l * RANK, RANK), RANK), :]
            for p in range(FARL // 2):
                j1, j2 = far_leaf[l, 2 * p], far_leaf[l, 2 * p + 1]
                rows = joined(
                    moved(skel_rows[j1 >> 1], j1, 0), moved(skel_rows[j2 >> 1], j2, 1)
                )
                high, low = far_tiles(feat, rows)
                far_high[l, :, 128 * p : 128 * (p + 1)] = high
                far_low[l, :, 128 * p : 128 * (p + 1)] = low
        far_leaves(lp, lambda j: gather1[j >> 4, 2 + ((j >> 1) & 7)])
        return carry

    def far_leaves(n, read):
        for q in range(2):
            lp = 2 * n + q
            parts = []
            for side in range(2):
                l = 2 * lp + side
                count = far_count[l]
                cols = []
                for p in range(FARL // 2):
                    s = 2 * p
                    j1, j2 = far_leaf[l, s], far_leaf[l, s + 1]
                    tile = joined(moved(read(j1), j1, 0), moved(read(j2), j2, 1))
                    slot = s + jnp.where(low_lanes, 0, 1)
                    cols.append(split2(jnp.where(slot < count, tile, 0.0)))
                c = jnp.concatenate(cols, axis=1)
                parts.append(dot_nt(far_high[l], c) + dot_nt(far_low[l], c))
            local[lp] = -FACTOR * fold(jnp.concatenate(parts, axis=0).T)

    def upper_matrix(buffer):
        def read_mid(m):
            return source_rows(buffer[m >> 4, m & 15, 1] - centre)

        for p in range(FARM // 2):
            one, two = read_mid(far_mid[0, 2 * p]), read_mid(far_mid[0, 2 * p + 1])
            high, low = far_tiles(mid_feat[0:RANK, :], joined(one, pltpu.roll(two, RANK, 1)))
            mid_high[:, 128 * p : 128 * (p + 1)] = high
            mid_low[:, 128 * p : 128 * (p + 1)] = low

        def read_top(j, want):
            return moved(source_rows(top_tiles[j >> 1] - centre), j, want)

        for p in range(2):
            j1 = far_top[0, 2 * p]
            j2 = far_top[0, min(2 * p + 1, FART - 1)]
            high, low = far_tiles(top_feat[0:RANK, :], joined(read_top(j1, 0), read_top(j2, 1)))
            top_high[:, 128 * p : 128 * (p + 1)] = high
            top_low[:, 128 * p : 128 * (p + 1)] = low

    def upper_local(read, read_top):
        cols = []
        for p in range(FARM // 2):
            m1, m2 = far_mid[0, 2 * p], far_mid[0, 2 * p + 1]
            cols.append(split2(joined(read(m1, 0), read(m2, 1))))
        c = jnp.concatenate(cols, axis=1)
        mid_far = -FACTOR * fold(dot_nt(c, mid_high[...]) + dot_nt(c, mid_low[...]))

        t0, t1, t2 = (read_top(far_top[0, s]) for s in range(FART))
        cols = [
            split2(joined(pltpu.roll(t0, RANK, 1), t1)),
            split2(joined(pltpu.roll(t2, RANK, 1), jnp.zeros((RHS, 128), F32))),
        ]
        c = jnp.concatenate(cols, axis=1)
        top_far = -FACTOR * fold(dot_nt(c, top_high[...]) + dot_nt(c, top_low[...]))
        high, low = halves(mid_transfer[0])
        t = split2(top_far)
        return mid_far + fold(dot(t, high) + dot(t, low))

    def down(read_mid, read_top):
        m = split2(upper_local(read_mid, read_top))
        for p in range(PER // 2):
            down_part = sum(dot(m, transfer2[part, :, 128 * p : 128 * (p + 1)]) for part in range(2))
            local[p] += fold(down_part)

    def finish(n, store):
        for t in range(4):
            l = 4 * n + t
            tile = local[2 * n + t // 2]
            c = split2(tile[:, RANK * (t % 2) : RANK * (t % 2 + 1)])
            far = fold(dot(c, basis_high[l]) + dot(c, basis_low[l]))
            near_part = -FACTOR * (fold(near_acc[l]) + tangent_part(l))
            store(l, near_part + far)

    lax.fori_loop(0, GSIZE, skeleton_rows, 0)
    lax.fori_loop(0, PER // 4, far_matrix, 0)
    wait_grp(all1, all_send, all_recv, 0)
    upper_matrix(all1)
    noise_value = noise[0]

    def first_leaves(n, carry):
        def store(l, value):
            cols = column(l)
            r = rhs[:, cols] - (noise_value * start[:, cols] + value)
            first[:, cols] = r
            halo2[1, :, cols] = r

        finish(n, store)
        return carry

    left, right = (slice(None), slice(0, width // 2)), (slice(None), slice(width // 2, width))
    def mid1(m, want):
        tile = all1[m >> 4, m & 15, 0]
        return pltpu.roll(tile, RANK, 1) if want else tile

    def top1(j):
        total = all1[j, 0, 0]
        for m in range(1, GSIZE):
            total += all1[j, m, 0]
        return total

    down(mid1, top1)
    lax.fori_loop(0, PER // 8, first_leaves, 0)
    launch(halo_copies(halo2, 1, *left))
    lax.fori_loop(PER // 8, PER // 4, first_leaves, 0)
    launch(halo_copies(halo2, 2, *right))

    coefficients(lambda leaf: first[:, LEAF * leaf : LEAF * (leaf + 1)], gather2.at[i], 0, mids2.at[i])
    launch(leaf_copies(mids2, sum_send, sum_recv, 1))
    launch(leaf_copies(gather2, coef_send, coef_recv, 1))
    field_moments(PER)
    for copy in halo_copies(halo2, 1, *left) + halo_copies(halo2, 2, *right):
        copy.wait_recv()

    def edge_fields(n, carry):
        for t in range(4):
            l = 4 * n + t
            for block in (0, 2):
                field[block * PER + l] = split2(halo2[block, :, column(l)])
        return carry

    lax.fori_loop(0, PER // 4, edge_fields, 0)
    field_moments(0)
    field_moments(2 * PER)

    def near_again(n, carry):
        multiply(n, 0)
        multiply(n, 1)
        return carry

    lax.fori_loop(0, PER // 4, near_again, 0)
    wait_leaf(mids2, sum_send, sum_recv, 1)
    group_top = jnp.zeros(tile_shape, F32)
    for p in range(GSIZE // 2):
        one, two = mids2[2 * p], mids2[2 * p + 1]
        all2[g, p] = joined(one, pltpu.roll(two, RANK, 1))
        group_top += one + two
    all2[g, GSIZE // 2] = group_top
    launch(grp_copies(all2, all_send, all_recv, 1))
    wait_leaf(gather2, coef_send, coef_recv, 1)

    def near_and_far(n, carry):
        multiply(PER // 4 + n, 0)
        multiply(PER // 4 + n, 1)
        far_leaves(n, lambda j: gather2[j >> 4, (j >> 1) & 7])
        return carry

    lax.fori_loop(0, PER // 4, near_and_far, 0)
    wait_grp(all2, all_send, all_recv, 1)

    def image_leaves(n, carry):
        def store(l, value):
            cols = column(l)
            image[:, cols] = noise_value * first[:, cols] + value

        finish(n, store)
        return carry

    down(
        lambda m, want: moved(all2[m >> 4, (m & 15) >> 1], m, want),
        lambda j: all2[j, GSIZE // 2],
    )
    lax.fori_loop(0, PER // 4, image_leaves, 0)

    dots = jnp.zeros((RHS, LEAF), F32)
    squares = jnp.zeros((RHS, LEAF), F32)
    for l in range(PER):
        cols = slice(LEAF * l, LEAF * (l + 1))
        y = image[:, cols]
        dots += first[:, cols] * y
        squares += y * y
    sums1[i] = jnp.where(
        low_lanes,
        jnp.sum(dots, axis=1, keepdims=True),
        jnp.sum(squares, axis=1, keepdims=True),
    )
    launch(leaf_copies(sums1, sum_send, sum_recv, 0))
    wait_leaf(sums1, sum_send, sum_recv, 0)
    total = sums1[0]
    for k in range(1, GSIZE):
        total += sums1[k]
    sums2[g] = total
    launch(grp_copies(sums2, tot_send, tot_recv, 0))
    wait_grp(sums2, tot_send, tot_recv, 0)
    total = sums2[0]
    for k in range(1, GROUPS):
        total += sums2[k]
    total = total / (LEAVES * LEAF)
    alpha = total[:, 0:1] / (total[:, RANK : RANK + 1] + 1e-6)
    step[...] = jnp.broadcast_to(alpha, (RHS, PER * LEAF))
    for copy in pending:
        copy.wait_send()


def shards(*args):
    smem = pl.BlockSpec(memory_space=pltpu.SMEM)
    vmem = pl.BlockSpec(memory_space=pltpu.VMEM)
    hbm = pl.BlockSpec(memory_space=pl.ANY)
    alphas, betas = tangent_tables()
    tables = (jnp.asarray(morton_table()), jnp.asarray(alphas), jnp.asarray(betas))
    out = jax.ShapeDtypeStruct((RHS, PER * LEAF), F32)
    tile = (8, 128)

    def buffer(shape, dtype=F32):
        return pltpu.VMEM(shape, dtype)

    def sems(*shape):
        return pltpu.SemaphoreType.DMA(shape)

    scratch = [
        buffer((PER // 2 * NEAR * LEAF, LEAF), BF),
        buffer((PER // 2 * NEAR * LEAF, LEAF), BF),
        buffer((PER, RANK, FARL * RANK), BF),
        buffer((PER, RANK, FARL * RANK), BF),
        buffer((RANK, FARM * RANK), BF),
        buffer((RANK, FARM * RANK), BF),
        buffer((RANK, 4 * RANK), BF),
        buffer((RANK, 4 * RANK), BF),
        buffer((3, 8, PER * LEAF + PACKED)),
        buffer((3, 8, PER * LEAF)),
        buffer((GSIZE, TILES1) + tile),
        buffer((GSIZE, TILES2) + tile),
        buffer((GSIZE,) + tile),
        buffer((GROUPS, GSIZE, 2) + tile),
        buffer((GROUPS, GSIZE // 2 + 1) + tile),
        buffer((GSIZE,) + tile),
        buffer((GROUPS,) + tile),
        buffer((WIN, 2 * RHS, LEAF), BF),
        buffer((WIN, LEAF, PIECES), BF),
        buffer((PER, PIECES, LEAF), BF),
        buffer((PER, 8, LEAF)),
        buffer((WIN, 2, RHS, 8)),
        buffer((GSIZE * PER // 2,) + tile),
        pltpu.SMEM((PER, NEAR), F32),
        pltpu.SMEM((PER, NEAR), F32),
        buffer((PER * RANK, PIECES), BF),
        buffer((128, PIECES), BF),
        buffer((128, PIECES), BF),
        buffer((GROUPS // 2,) + tile),
        buffer((PER, RANK, LEAF), BF),
        buffer((PER, RANK, LEAF), BF),
        buffer((2, RANK, PER * RANK), BF),
        buffer((PER, 2 * RHS, LEAF)),
        buffer((PER // 2,) + tile),
        buffer((RHS, PER * LEAF)),
        buffer((PER, RANK, LEAF)),
        buffer((PER, RANK, RANK)),
        sems(3),
        sems(3, 2),
        sems(3, 2),
        sems(2, GSIZE),
        sems(2, GSIZE),
        sems(2, GROUPS),
        sems(2, GROUPS),
        sems(2, GSIZE),
        sems(2, GSIZE),
        sems(1, GROUPS),
        sems(1, GROUPS),
    ]
    first, image, step = pl.pallas_call(
        body,
        out_shape=(out, out, out),
        in_specs=[hbm if n in (1, 6, 7) else vmem for n in range(9)] + [smem] * 10,
        out_specs=(vmem, vmem, vmem),
        scratch_shapes=scratch,
        compiler_params=pltpu.CompilerParams(
            collective_id=0, has_side_effects=True, vmem_limit_bytes=61 << 20
        ),
    )(*args, *tables)
    return args[2] + step * first, first - step * image


def solution(mesh):
    columns = P(None, ("grp", "leaf"))
    blocks = P(("grp", "leaf"), None, None)
    lists = P(("grp", "leaf"), None)
    return jax.shard_map(
        shards,
        mesh=mesh,
        in_specs=(
            columns,
            columns,
            columns,
            columns,
            columns,
            P(),
            blocks,
            blocks,
            blocks,
            P(),
            lists,
            P(("grp", "leaf")),
            lists,
            P(("grp", "leaf")),
            lists,
            P("grp", None),
        ),
        out_specs=(columns, columns),
        check_vma=False,
    )
```

```python
import functools
import math

import jax
import jax.numpy as jnp
import numpy as np
from jax import lax
from jax.experimental import pallas as pl
from jax.experimental.pallas import tpu as pltpu
from jax.sharding import PartitionSpec as P

BF = jnp.bfloat16
F32 = jnp.float32
MESH = pl.DeviceIdType.MESH
NT = (((1,), (1,)), ((), ()))

LEAF = 256
RANK = 64
RHS = 8
PER = 16
NEAR = 16
FARL = 32
FARM = 16
FART = 3
GROUPS = 8
GSIZE = 16
LEAVES = 2048
WIN = 3 * PER
PIECES = 48
TILES1 = 5 + PER // 2
TILES2 = PER // 2
PACKED = 3 * PER * LEAF // 8

LOG2E = math.log2(math.e)
KAPPA = 0.75 * LOG2E * LOG2E
FACTOR = math.e * math.log(2.0)
TINY = 1e-30


def morton_table():
    ids = np.arange(LEAVES)
    coords = [np.zeros_like(ids) for _ in range(3)]
    for bit in range(30):
        coords[bit % 3] += ((ids >> bit) & 1) << (bit // 3)
    packed = coords[0] + 256 * coords[1] + 65536 * coords[2]
    return np.pad(packed, (PER, PER)).astype(np.int32)


def tangent_tables():
    mean = 0.75 * (np.arange(512) + 0.5)
    s = np.sqrt(mean)
    beta = 0.5 * np.exp(-s) / (LOG2E * LOG2E) / FACTOR
    alpha = -(1 + s) * np.exp(-s) / FACTOR - beta * mean * LOG2E * LOG2E
    alpha = np.append(alpha, -LOG2E)
    return alpha.astype(np.float32), beta.astype(np.float32)


def rounded(x):
    return x.astype(BF).astype(F32)


def split2(x):
    high = rounded(x)
    return jnp.concatenate([high, x - high], axis=0).astype(BF)


def split3(x):
    first = rounded(x)
    rest = x - first
    second = rounded(rest)
    return first, second, rounded(rest - second)


def source_pieces(w):
    a, b, c = split3(w)
    return jnp.concatenate([a, b, a, b, c, a], axis=0)


def target_pieces(u):
    a, b, c = split3(u)
    return jnp.concatenate([a, a, b, b, a, c], axis=0)


def rows_of(shape):
    return lax.broadcasted_iota(jnp.int32, shape, 0)


def source_rows(x):
    row = rows_of(x.shape)
    x = jnp.where(row < 3, x, 0.0)
    norm = KAPPA * jnp.sum(x * x, axis=0, keepdims=True)
    return jnp.where(row == 3, norm, jnp.where(row == 4, 1.0, x))


def target_rows(x):
    row = rows_of(x.shape)
    x = jnp.where(row < 3, x, 0.0)
    norm = KAPPA * jnp.sum(x * x, axis=0, keepdims=True)
    return jnp.where(row == 4, norm, jnp.where(row == 3, 1.0, (-2.0 * KAPPA) * x))


def kernel_value(q, shift):
    y = shift - q * lax.rsqrt(q)
    return y * jnp.exp2(y)


def halves(x):
    high = x.astype(BF)
    return high, (x - high.astype(F32)).astype(BF)


def dot(a, b):
    return jnp.dot(a, b, preferred_element_type=F32)


def dot_nt(a, b):
    return lax.dot_general(a, b, NT, preferred_element_type=F32)


def fold(x):
    return x[:RHS] + x[RHS:]


def body(
    points,
    rhs_hbm,
    start,
    leaf_skel,
    mid_skel,
    top_skel,
    basis_hbm,
    transfer_hbm,
    mid_transfer,
    noise,
    near,
    near_count,
    far_leaf,
    far_count,
    far_mid,
    far_top,
    corners,
    alphas,
    betas,
    first,
    image,
    step,
    remainder0,
    remainder1,
    far_high,
    far_low,
    mid_high,
    mid_low,
    top_high,
    top_low,
    halo1,
    halo2,
    gather1,
    gather2,
    mids2,
    all1,
    all2,
    sums1,
    sums2,
    field,
    wfeat,
    ufeat,
    urows,
    moments,
    skel_rows,
    tangent_a,
    tangent_b,
    skel_feat,
    mid_feat,
    top_feat,
    top_tiles,
    basis_high,
    basis_low,
    transfer2,
    near_acc,
    local,
    rhs,
    basis,
    transfer,
    fetch_sem,
    halo_send,
    halo_recv,
    coef_send,
    coef_recv,
    all_send,
    all_recv,
    sum_send,
    sum_recv,
    tot_send,
    tot_recv,
):
    g = lax.axis_index("grp")
    i = lax.axis_index("leaf")
    lane = lax.broadcasted_iota(jnp.int32, (RHS, 128), 1)
    low_lanes = lane < RANK
    tile_shape = (RHS, 128)

    def peer_leaf(k):
        return (g, lax.rem(i + k, GSIZE))

    def peer_grp(k):
        return (lax.rem(g + k, GROUPS), i)

    up = i + 1
    down = i + GSIZE - 1
    after = (lax.rem(g + lax.div(up, GSIZE), GROUPS), lax.rem(up, GSIZE))
    before = (lax.rem(g + GROUPS - 1 + lax.div(down, GSIZE), GROUPS), lax.rem(down, GSIZE))

    fetches = [
        pltpu.make_async_copy(src, dst, fetch_sem.at[n])
        for n, (src, dst) in enumerate(
            ((basis_hbm, basis), (transfer_hbm, transfer), (rhs_hbm, rhs))
        )
    ]
    for copy in fetches:
        copy.start()
    barrier = pltpu.get_barrier_semaphore()
    partners = (
        [peer_leaf(k) for k in range(1, GSIZE)]
        + [peer_grp(k) for k in range(1, GROUPS)]
        + [after, before]
    )
    for partner in partners:
        pl.semaphore_signal(barrier, inc=1, device_id=partner, device_id_type=MESH)

    def remote(src, dst, send, recv, device):
        return pltpu.make_async_remote_copy(
            src_ref=src,
            dst_ref=dst,
            send_sem=send,
            recv_sem=recv,
            device_id=device,
            device_id_type=MESH,
        )

    def halo_copies(window, phase, *where):
        own, low, high = (window.at[(block,) + where] for block in (1, 0, 2))
        return [
            remote(own, low, halo_send.at[phase, 0], halo_recv.at[phase, 0], after),
            remote(own, high, halo_send.at[phase, 1], halo_recv.at[phase, 1], before),
        ]

    def leaf_copies(buffer, send, recv, phase):
        own = buffer.at[i]
        return [
            remote(own, own, send.at[phase, k], recv.at[phase, i], peer_leaf(k))
            for k in range(1, GSIZE)
        ]

    def wait_leaf(buffer, send, recv, phase):
        for k in range(1, GSIZE):
            src = lax.rem(i + k, GSIZE)
            theirs = buffer.at[src]
            remote(theirs, theirs, send.at[phase, k], recv.at[phase, src], peer_leaf(k)).wait_recv()

    def grp_copies(buffer, send, recv, phase):
        return [
            remote(buffer.at[g], buffer.at[g], send.at[phase, k], recv.at[phase, g], peer_grp(k))
            for k in range(1, GROUPS)
        ]

    def wait_grp(buffer, send, recv, phase):
        for k in range(1, GROUPS):
            src = lax.rem(g + k, GROUPS)
            remote(
                buffer.at[src], buffer.at[src], send.at[phase, k], recv.at[phase, src], peer_grp(k)
            ).wait_recv()

    pending = []

    def launch(copies):
        for copy in copies:
            copy.start()
        pending.extend(copies)

    def coefficients(read, tiles, first_tile, mid_tile):
        total = jnp.zeros((2 * RHS, RANK), F32)
        for p in range(PER // 2):
            parts = []
            for side in range(2):
                leaf = 2 * p + side
                v = split2(read(leaf))
                field[PER + leaf] = v
                parts.append(fold(dot_nt(v, basis_high[leaf]) + dot_nt(v, basis_low[leaf])))
            tile = jnp.concatenate(parts, axis=1)
            tiles[first_tile + p] = tile
            c = split2(tile)
            for part in range(2):
                total += dot_nt(c, transfer2[part, :, 128 * p : 128 * (p + 1)])
        mid = fold(total)
        m = split2(mid)
        high, low = halves(mid_transfer[0])
        top = fold(dot_nt(m, high) + dot_nt(m, low))
        mid_tile[...] = jnp.concatenate([mid, top], axis=1)

    def column(leaf):
        return pl.ds(pl.multiple_of(leaf * LEAF, LEAF), LEAF)

    width, span = PER * LEAF, PACKED // 3
    halo1[1, :, 0:width] = start[...]
    for c in range(3):
        for r in range(8):
            halo1[1, r : r + 1, width + c * span : width + (c + 1) * span] = points[
                c : c + 1, r * span : (r + 1) * span
            ]
    for copy in fetches:
        copy.wait()
    for leaf in range(PER):
        high, low = halves(basis[leaf])
        basis_high[leaf] = high
        basis_low[leaf] = low
    for p in range(PER // 2):
        both = jnp.concatenate([transfer[2 * p], transfer[2 * p + 1]], axis=1)
        high, low = halves(both)
        transfer2[0, :, 128 * p : 128 * (p + 1)] = high
        transfer2[1, :, 128 * p : 128 * (p + 1)] = low
    pl.semaphore_wait(barrier, len(partners))
    launch(halo_copies(halo1, 0))

    own_gather = gather1.at[i]
    own_skel = []
    for p in range(PER // 2):
        tile = jnp.concatenate(
            [leaf_skel[:, 128 * p : 128 * (p + 1)], jnp.zeros((5, 128), F32)], axis=0
        )
        own_skel.append(tile)
        own_gather[2 + PER // 2 : 5 + PER // 2, p : p + 1, :] = tile[0:3].reshape(3, 1, 128)
    own_gather[1] = jnp.zeros((8, 128), F32)
    own_gather[1, 0:3, 0:RANK] = mid_skel[...]
    coefficients(lambda leaf: start[:, LEAF * leaf : LEAF * (leaf + 1)], own_gather, 2, own_gather.at[0])
    centre = jnp.concatenate([jnp.floor(points[:, 0:1]), jnp.zeros((5, 1), F32)], axis=0)
    device = g * GSIZE + i
    base = device * PER

    def leaf_points(block, l):
        per_row = span // LEAF
        row, place = lax.div(l, per_row), lax.rem(l, per_row) * LEAF
        out = jnp.zeros((8, LEAF), F32)
        for c in range(3):
            cols = pl.ds(pl.multiple_of(width + c * span + place, LEAF), LEAF)
            out = jnp.where(rows_of((8, LEAF)) == c, halo1[block, pl.ds(row, 1), cols], out)
        return out

    def window_features(leaf, block, place):
        x = leaf_points(block, place) - centre
        wfeat[leaf] = source_pieces(source_rows(x)).T.astype(BF)
        return x

    def tangents(l):
        a = corners[base + PER + l] + 0x202020
        count = near_count[l]
        for s in range(NEAR):
            d = a - corners[base + near[l, s]]
            dx = (d & 255) - 32
            dy = ((d >> 8) & 255) - 32
            dz = (d >> 16) - 32
            d2 = jnp.minimum(dx * dx + dy * dy + dz * dz, 511)
            live = s < count
            tangent_a[l, s] = jnp.where(live, alphas[d2], 0.0)
            tangent_b[l, s] = jnp.where(live, betas[d2], 0.0)

    def own_features(n, carry):
        for t in range(4):
            l = 4 * n + t
            x = window_features(PER + l, 1, l)
            u = target_rows(x)
            urows[l] = u
            ufeat[l] = target_pieces(u).astype(BF)
            tangents(l)
        return carry

    lax.fori_loop(0, PER // 4, own_features, 0)
    for p in range(PER // 2):
        u = target_pieces(target_rows(own_skel[p] - centre))
        skel_feat[128 * p : 128 * (p + 1), :] = u.T.astype(BF)
    u = target_pieces(target_rows(own_gather[1] - centre))
    mid_feat[...] = u.T.astype(BF)
    for p in range(GROUPS // 2):
        top_tiles[p] = jnp.concatenate(
            [top_skel[:, 128 * p : 128 * (p + 1)], jnp.zeros((5, 128), F32)], axis=0
        )
    tile = top_tiles[lax.div(g, 2)]
    tile = jnp.where(lax.rem(g, 2) == 0, tile, pltpu.roll(tile, RANK, 1))
    top_feat[...] = target_pieces(target_rows(tile - centre)).T.astype(BF)

    def field_moments(*first_leaves):
        lane8 = lax.broadcasted_iota(jnp.int32, (RHS, 8), 1)

        def some(n, carry):
            for leaf in (first + 8 * n + t for t in range(8) for first in first_leaves):
                r = fold(dot(field[leaf], wfeat[leaf]))
                m = r[:, 0:8] + r[:, 8:16] + r[:, 32:40]
                moments[leaf, 0] = m
                moments[leaf, 1] = jnp.where(lane8 == 3, m[:, 4:5], 0.0)
            return carry

        lax.fori_loop(0, PER // 8, some, 0)

    field_moments(PER)
    for copy in halo_copies(halo1, 0):
        copy.wait_recv()
    launch(leaf_copies(gather1, coef_send, coef_recv, 0))

    def edge_features(n, carry):
        for t in range(4):
            l = 4 * n + t
            for block in (0, 2):
                leaf = block * PER + l
                window_features(leaf, block, l)
                field[leaf] = split2(halo1[block, :, column(l)])
        return carry

    lax.fori_loop(0, PER // 4, edge_features, 0)
    field_moments(0, 2 * PER)

    shift = alphas[512]
    remainders = (remainder0, remainder1)

    def evaluate(n, side):
        l = 2 * n + side
        feat = ufeat[l]
        for c in range(0, LEAF, 64):
            for t in range(NEAR):
                q = jnp.maximum(dot(wfeat[near[l, t], c : c + 64, :], feat), TINY)
                r = kernel_value(q, shift) - (q * tangent_b[l, t] + tangent_a[l, t])
                row = (n * NEAR + t) * LEAF + c
                remainders[side][pl.ds(pl.multiple_of(row, 64), 64), :] = r.astype(BF)

    def multiply(n, side):
        l = 2 * n + side
        cols = []
        live = near_count[l]
        for t in range(NEAR):
            v = field[near[l, t]]
            cols.append(jnp.where(t < live, v, jnp.zeros_like(v)))
        rows = pl.ds(pl.multiple_of(n * NEAR * LEAF, LEAF), NEAR * LEAF)
        near_acc[l] = dot(jnp.concatenate(cols, axis=1), remainders[side][rows, :])

    def tangent_part(l):
        total = jnp.zeros((RHS, 8), F32)
        for s in range(NEAR):
            j = near[l, s]
            total += tangent_b[l, s] * moments[j, 0] + tangent_a[l, s] * moments[j, 1]
        out = total[:, 0:1] * urows[l, 0:1, :]
        for k in range(1, 5):
            out += total[:, k : k + 1] * urows[l, k : k + 1, :]
        return out

    remainder1[(PER // 2 - 1) * NEAR * LEAF :, :] = jnp.zeros((NEAR * LEAF, LEAF), BF)

    def near_step(n, carry):
        multiply(lax.rem(n + PER // 2 - 1, PER // 2), 1)
        evaluate(n, 0)
        multiply(n, 0)
        evaluate(n, 1)
        return carry

    lax.fori_loop(0, PER // 4, near_step, 0)
    wait_leaf(gather1, coef_send, coef_recv, 0)
    for m in range(GSIZE):
        all1[g, m] = gather1[m, 0:2]
    launch(grp_copies(all1, all_send, all_recv, 0))
    lax.fori_loop(PER // 4, PER // 2, near_step, 0)
    multiply(PER // 2 - 1, 1)

    def moved(tile, index, want):
        return jnp.where((index & 1) == want, tile, pltpu.roll(tile, RANK, 1))

    def joined(first_tile, second_tile):
        return jnp.where(low_lanes, first_tile, second_tile)

    def far_tiles(feat, rows):
        q = jnp.maximum(dot(feat, source_pieces(rows).astype(BF)), TINY)
        return halves(kernel_value(q, shift))

    def skeleton_rows(n, carry):
        for t in range(PER // 2):
            parts = [gather1[n, 2 + PER // 2 + c, t : t + 1, :] for c in range(3)]
            tile = jnp.concatenate(parts + [jnp.zeros((5, 128), F32)], axis=0)
            skel_rows[n * (PER // 2) + t] = source_rows(tile - centre)
        return carry

    def far_matrix(lp, carry):
        for side in range(4):
            l = 4 * lp + side
            feat = skel_feat[pl.ds(pl.multiple_of(l * RANK, RANK), RANK), :]
            for p in range(FARL // 2):
                j1, j2 = far_leaf[l, 2 * p], far_leaf[l, 2 * p + 1]
                rows = joined(
                    moved(skel_rows[j1 >> 1], j1, 0), moved(skel_rows[j2 >> 1], j2, 1)
                )
                high, low = far_tiles(feat, rows)
                far_high[l, :, 128 * p : 128 * (p + 1)] = high
                far_low[l, :, 128 * p : 128 * (p + 1)] = low
        far_leaves(lp, lambda j: gather1[j >> 4, 2 + ((j >> 1) & 7)])
        return carry

    def far_leaves(n, read):
        for q in range(2):
            lp = 2 * n + q
            parts = []
            for side in range(2):
                l = 2 * lp + side
                count = far_count[l]
                cols = []
                for p in range(FARL // 2):
                    s = 2 * p
                    j1, j2 = far_leaf[l, s], far_leaf[l, s + 1]
                    tile = joined(moved(read(j1), j1, 0), moved(read(j2), j2, 1))
                    slot = s + jnp.where(low_lanes, 0, 1)
                    cols.append(split2(jnp.where(slot < count, tile, 0.0)))
                c = jnp.concatenate(cols, axis=1)
                parts.append(dot_nt(far_high[l], c) + dot_nt(far_low[l], c))
            local[lp] = -FACTOR * fold(jnp.concatenate(parts, axis=0).T)

    def upper_matrix(buffer):
        def read_mid(m):
            return source_rows(buffer[m >> 4, m & 15, 1] - centre)

        for p in range(FARM // 2):
            one, two = read_mid(far_mid[0, 2 * p]), read_mid(far_mid[0, 2 * p + 1])
            high, low = far_tiles(mid_feat[0:RANK, :], joined(one, pltpu.roll(two, RANK, 1)))
            mid_high[:, 128 * p : 128 * (p + 1)] = high
            mid_low[:, 128 * p : 128 * (p + 1)] = low

        def read_top(j, want):
            return moved(source_rows(top_tiles[j >> 1] - centre), j, want)

        for p in range(2):
            j1 = far_top[0, 2 * p]
            j2 = far_top[0, min(2 * p + 1, FART - 1)]
            high, low = far_tiles(top_feat[0:RANK, :], joined(read_top(j1, 0), read_top(j2, 1)))
            top_high[:, 128 * p : 128 * (p + 1)] = high
            top_low[:, 128 * p : 128 * (p + 1)] = low

    def upper_local(read, read_top):
        cols = []
        for p in range(FARM // 2):
            m1, m2 = far_mid[0, 2 * p], far_mid[0, 2 * p + 1]
            cols.append(split2(joined(read(m1, 0), read(m2, 1))))
        c = jnp.concatenate(cols, axis=1)
        mid_far = -FACTOR * fold(dot_nt(c, mid_high[...]) + dot_nt(c, mid_low[...]))

        t0, t1, t2 = (read_top(far_top[0, s]) for s in range(FART))
        cols = [
            split2(joined(pltpu.roll(t0, RANK, 1), t1)),
            split2(joined(pltpu.roll(t2, RANK, 1), jnp.zeros((RHS, 128), F32))),
        ]
        c = jnp.concatenate(cols, axis=1)
        top_far = -FACTOR * fold(dot_nt(c, top_high[...]) + dot_nt(c, top_low[...]))
        high, low = halves(mid_transfer[0])
        t = split2(top_far)
        return mid_far + fold(dot(t, high) + dot(t, low))

    def down(read_mid, read_top):
        m = split2(upper_local(read_mid, read_top))
        for p in range(PER // 2):
            down_part = sum(dot(m, transfer2[part, :, 128 * p : 128 * (p + 1)]) for part in range(2))
            local[p] += fold(down_part)

    def finish(n, store):
        for t in range(4):
            l = 4 * n + t
            tile = local[2 * n + t // 2]
            c = split2(tile[:, RANK * (t % 2) : RANK * (t % 2 + 1)])
            far = fold(dot(c, basis_high[l]) + dot(c, basis_low[l]))
            near_part = -FACTOR * (fold(near_acc[l]) + tangent_part(l))
            store(l, near_part + far)

    lax.fori_loop(0, GSIZE, skeleton_rows, 0)
    lax.fori_loop(0, PER // 4, far_matrix, 0)
    wait_grp(all1, all_send, all_recv, 0)
    upper_matrix(all1)
    noise_value = noise[0]

    def first_leaves(n, carry):
        def store(l, value):
            cols = column(l)
            r = rhs[:, cols] - (noise_value * start[:, cols] + value)
            first[:, cols] = r
            halo2[1, :, cols] = r

        finish(n, store)
        return carry

    left, right = (slice(None), slice(0, width // 2)), (slice(None), slice(width // 2, width))
    def mid1(m, want):
        tile = all1[m >> 4, m & 15, 0]
        return pltpu.roll(tile, RANK, 1) if want else tile

    def top1(j):
        total = all1[j, 0, 0]
        for m in range(1, GSIZE):
            total += all1[j, m, 0]
        return total

    down(mid1, top1)
    lax.fori_loop(0, PER // 8, first_leaves, 0)
    launch(halo_copies(halo2, 1, *left))
    lax.fori_loop(PER // 8, PER // 4, first_leaves, 0)
    launch(halo_copies(halo2, 2, *right))

    coefficients(lambda leaf: first[:, LEAF * leaf : LEAF * (leaf + 1)], gather2.at[i], 0, mids2.at[i])
    launch(leaf_copies(mids2, sum_send, sum_recv, 1))
    launch(leaf_copies(gather2, coef_send, coef_recv, 1))
    field_moments(PER)
    for copy in halo_copies(halo2, 1, *left) + halo_copies(halo2, 2, *right):
        copy.wait_recv()

    def edge_fields(n, carry):
        for t in range(4):
            l = 4 * n + t
            for block in (0, 2):
                field[block * PER + l] = split2(halo2[block, :, column(l)])
        return carry

    lax.fori_loop(0, PER // 4, edge_fields, 0)
    field_moments(0, 2 * PER)

    def near_again(n, carry):
        multiply(n, 0)
        multiply(n, 1)
        return carry

    lax.fori_loop(0, PER // 4, near_again, 0)
    wait_leaf(mids2, sum_send, sum_recv, 1)
    group_top = jnp.zeros(tile_shape, F32)
    for p in range(GSIZE // 2):
        one, two = mids2[2 * p], mids2[2 * p + 1]
        all2[g, p] = joined(one, pltpu.roll(two, RANK, 1))
        group_top += one + two
    all2[g, GSIZE // 2] = group_top
    launch(grp_copies(all2, all_send, all_recv, 1))
    wait_leaf(gather2, coef_send, coef_recv, 1)

    def near_and_far(n, carry):
        multiply(PER // 4 + n, 0)
        multiply(PER // 4 + n, 1)
        far_leaves(n, lambda j: gather2[j >> 4, (j >> 1) & 7])
        return carry

    lax.fori_loop(0, PER // 4, near_and_far, 0)
    wait_grp(all2, all_send, all_recv, 1)

    def image_leaves(n, carry):
        def store(l, value):
            cols = column(l)
            image[:, cols] = noise_value * first[:, cols] + value

        finish(n, store)
        return carry

    down(
        lambda m, want: moved(all2[m >> 4, (m & 15) >> 1], m, want),
        lambda j: all2[j, GSIZE // 2],
    )
    lax.fori_loop(0, PER // 4, image_leaves, 0)

    dots = jnp.zeros((RHS, LEAF), F32)
    squares = jnp.zeros((RHS, LEAF), F32)
    for l in range(PER):
        cols = slice(LEAF * l, LEAF * (l + 1))
        y = image[:, cols]
        dots += first[:, cols] * y
        squares += y * y
    sums1[i] = jnp.where(
        low_lanes,
        jnp.sum(dots, axis=1, keepdims=True),
        jnp.sum(squares, axis=1, keepdims=True),
    )
    launch(leaf_copies(sums1, sum_send, sum_recv, 0))
    wait_leaf(sums1, sum_send, sum_recv, 0)
    total = sums1[0]
    for k in range(1, GSIZE):
        total += sums1[k]
    sums2[g] = total
    launch(grp_copies(sums2, tot_send, tot_recv, 0))
    wait_grp(sums2, tot_send, tot_recv, 0)
    total = sums2[0]
    for k in range(1, GROUPS):
        total += sums2[k]
    total = total / (LEAVES * LEAF)
    alpha = total[:, 0:1] / (total[:, RANK : RANK + 1] + 1e-6)
    step[...] = jnp.broadcast_to(alpha, (RHS, PER * LEAF))
    for copy in pending:
        copy.wait_send()


def shards(*args):
    smem = pl.BlockSpec(memory_space=pltpu.SMEM)
    vmem = pl.BlockSpec(memory_space=pltpu.VMEM)
    hbm = pl.BlockSpec(memory_space=pl.ANY)
    alphas, betas = tangent_tables()
    tables = (jnp.asarray(morton_table()), jnp.asarray(alphas), jnp.asarray(betas))
    out = jax.ShapeDtypeStruct((RHS, PER * LEAF), F32)
    tile = (8, 128)

    def buffer(shape, dtype=F32):
        return pltpu.VMEM(shape, dtype)

    def sems(*shape):
        return pltpu.SemaphoreType.DMA(shape)

    scratch = [
        buffer((PER // 2 * NEAR * LEAF, LEAF), BF),
        buffer((PER // 2 * NEAR * LEAF, LEAF), BF),
        buffer((PER, RANK, FARL * RANK), BF),
        buffer((PER, RANK, FARL * RANK), BF),
        buffer((RANK, FARM * RANK), BF),
        buffer((RANK, FARM * RANK), BF),
        buffer((RANK, 4 * RANK), BF),
        buffer((RANK, 4 * RANK), BF),
        buffer((3, 8, PER * LEAF + PACKED)),
        buffer((3, 8, PER * LEAF)),
        buffer((GSIZE, TILES1) + tile),
        buffer((GSIZE, TILES2) + tile),
        buffer((GSIZE,) + tile),
        buffer((GROUPS, GSIZE, 2) + tile),
        buffer((GROUPS, GSIZE // 2 + 1) + tile),
        buffer((GSIZE,) + tile),
        buffer((GROUPS,) + tile),
        buffer((WIN, 2 * RHS, LEAF), BF),
        buffer((WIN, LEAF, PIECES), BF),
        buffer((PER, PIECES, LEAF), BF),
        buffer((PER, 8, LEAF)),
        buffer((WIN, 2, RHS, 8)),
        buffer((GSIZE * PER // 2,) + tile),
        pltpu.SMEM((PER, NEAR), F32),
        pltpu.SMEM((PER, NEAR), F32),
        buffer((PER * RANK, PIECES), BF),
        buffer((128, PIECES), BF),
        buffer((128, PIECES), BF),
        buffer((GROUPS // 2,) + tile),
        buffer((PER, RANK, LEAF), BF),
        buffer((PER, RANK, LEAF), BF),
        buffer((2, RANK, PER * RANK), BF),
        buffer((PER, 2 * RHS, LEAF)),
        buffer((PER // 2,) + tile),
        buffer((RHS, PER * LEAF)),
        buffer((PER, RANK, LEAF)),
        buffer((PER, RANK, RANK)),
        sems(3),
        sems(3, 2),
        sems(3, 2),
        sems(2, GSIZE),
        sems(2, GSIZE),
        sems(2, GROUPS),
        sems(2, GROUPS),
        sems(2, GSIZE),
        sems(2, GSIZE),
        sems(1, GROUPS),
        sems(1, GROUPS),
    ]
    first, image, step = pl.pallas_call(
        body,
        out_shape=(out, out, out),
        in_specs=[hbm if n in (1, 6, 7) else vmem for n in range(9)] + [smem] * 10,
        out_specs=(vmem, vmem, vmem),
        scratch_shapes=scratch,
        compiler_params=pltpu.CompilerParams(
            collective_id=0, has_side_effects=True, vmem_limit_bytes=61 << 20
        ),
    )(*args, *tables)
    return args[2] + step * first, first - step * image


def solution(mesh):
    columns = P(None, ("grp", "leaf"))
    blocks = P(("grp", "leaf"), None, None)
    lists = P(("grp", "leaf"), None)
    return jax.shard_map(
        shards,
        mesh=mesh,
        in_specs=(
            columns,
            columns,
            columns,
            columns,
            columns,
            P(),
            blocks,
            blocks,
            blocks,
            P(),
            lists,
            P(("grp", "leaf")),
            lists,
            P(("grp", "leaf")),
            lists,
            P("grp", None),
        ),
        out_specs=(columns, columns),
        check_vma=False,
    )
```
